512 devices in a mesh: dp: 16 (over y, x_lo), seq: 32 (over x_hi, z, core).
Axes of the slice: x: 4 (x_hi: 2, x_lo: 2; x = x_hi * 2 + x_lo), y: 8, z: 8, core: 2. Of those that a mesh axis runs over, the one named last changes fastest.
Arguments:
- q_spatial: bfloat16 [16, 4096, 1536], P('dp', 'seq'), may hold values from -6 to 6
- k_spatial: bfloat16 [16, 4096, 1536], P('dp', 'seq'), may hold values from -6 to 6
- v_spatial: bfloat16 [16, 4096, 1536], P('dp', 'seq'), may hold values from -6 to 6
- q_temporal: bfloat16 [16, 4096, 1536], P('dp', 'seq'), may hold values from -6 to 6
- k_temporal: bfloat16 [16, 4096, 1536], P('dp', 'seq'), may hold values from -6 to 6
- v_temporal: bfloat16 [16, 4096, 1536], P('dp', 'seq'), may hold values from -6 to 6
- upstream: bfloat16 [16, 4096, 1536], P('dp', 'seq'), may hold values from -13.5 to 13.5
- norm_gains: float32 [4, 128], replicated, may hold values from 0.7 to 5
Outputs:
- grad_q_spatial: bfloat16 [16, 4096, 1536], P('dp', 'seq')
- grad_k_spatial: bfloat16 [16, 4096, 1536], P('dp', 'seq')
- grad_v_spatial: bfloat16 [16, 4096, 1536], P('dp', 'seq')
- grad_q_temporal: bfloat16 [16, 4096, 1536], P('dp', 'seq')
- grad_k_temporal: bfloat16 [16, 4096, 1536], P('dp', 'seq')
- grad_v_temporal: bfloat16 [16, 4096, 1536], P('dp', 'seq')
- gain_grads: float32 [4, 128], replicated
The draws below stay inside these ranges and needn't reach their ends.
All inputs are finite; a program needn't handle non-finite values.
Results may differ from the reference program's by a relative error of at most 0.013.
The reference program's roundings to bfloat16 on the way count: a program that leaves them out, or rounds other values in their place, can miss the bound.
Values may be sent and summed in bfloat16 or wider, within the bound.
No kernel may reach another device: no remote copies, remote signals or barrier semaphores. Data moves between devices by JAX's collectives and lax.ppermute only.
A program may use at most 128 MiB of HBM per device.

```python
import jax
import jax.numpy as jnp
from jax import lax

HEADS = 12
HEAD_DIM = 128
WIDTH = 1536
FRAMES = 4
S_FRAME = 1024
TOKENS_CLIP = 4096
CLIPS = 16


def base_normal(key, salt):
    values = jax.random.normal(jax.random.fold_in(key, salt), (CLIPS, TOKENS_CLIP, WIDTH), jnp.float32)
    return jnp.clip(values, -6.0, 6.0)


def draw_q_spatial(key, part):
    key = jax.random.fold_in(key, 1)
    own_rows = jnp.clip(jax.random.normal(key, (CLIPS, TOKENS_CLIP, WIDTH), jnp.float32), -6.0, 6.0)
    return own_rows.astype(jnp.bfloat16)


def draw_k_spatial(key, part):
    shared = base_normal(key, 500)
    return shared.astype(jnp.bfloat16)


def draw_q_temporal(key, part):
    key = jax.random.fold_in(key, 3)
    own_rows = jnp.clip(jax.random.normal(key, (CLIPS, TOKENS_CLIP, WIDTH), jnp.float32), -6.0, 6.0)
    return own_rows.astype(jnp.bfloat16)


def draw_k_temporal(key, part):
    shared = base_normal(key, 600)
    return shared.astype(jnp.bfloat16)


def draw_upstream(key, part):
    key = jax.random.fold_in(key, 7)
    clip_ramp = jnp.arange(CLIPS, dtype=jnp.float32) / max(CLIPS - 1, 1)
    token_ramp = jnp.arange(TOKENS_CLIP, dtype=jnp.float32) / max(TOKENS_CLIP - 1, 1)
    softmax_scale = (1.0 + 2.0 * clip_ramp)[:, None, None] * (1.0 + 2.0 * token_ramp)[None, :, None] / 4.0
    values = jnp.clip(jax.random.normal(key, (CLIPS, TOKENS_CLIP, WIDTH), jnp.float32), -6.0, 6.0)
    return (values * softmax_scale).astype(jnp.bfloat16)


def draw_norm_gains(key, part):
    key = jax.random.fold_in(key, 9)
    return jax.random.uniform(key, (4, HEAD_DIM), jnp.float32, 0.7, 1.4)


def level_of(key, dims, split, smallest, largest):
    factor_of = 1.0
    for dim, shards_of in split:
        heights = jax.random.uniform(jax.random.fold_in(jax.random.fold_in(key, 6), dim), (shards_of,), jnp.float32, smallest / len(split), largest / len(split))
        factor_of = factor_of * jnp.repeat(jnp.exp(heights), dims[dim] // shards_of).reshape((-1,) + (1,) * (len(dims) - 1 - dim))
    return factor_of


def scatter_about(own_key, dims, scale, limit, split=(), held_as=jnp.bfloat16):
    values = scale * jax.random.normal(own_key, dims, jnp.float32)
    if split:
        values = values * level_of(own_key, dims, split, -0.22, 0.18)
    return jnp.clip(values, -limit, limit).astype(held_as)


def setup_inputs(seed: int = 0) -> dict:
    keys = jax.random.split(jax.random.key(seed), 9)
    q_spatial = draw_q_spatial(jax.random.fold_in(keys[8], 71), 0)
    k_spatial = draw_k_spatial(jax.random.fold_in(keys[8], 71), 0)
    v_spatial = scatter_about(keys[2], (CLIPS, TOKENS_CLIP, WIDTH), 1.0, 6.0, ((0, 16), (1, 32)))
    q_temporal = draw_q_temporal(jax.random.fold_in(keys[8], 71), 0)
    k_temporal = draw_k_temporal(jax.random.fold_in(keys[8], 71), 0)
    v_temporal = scatter_about(keys[5], (CLIPS, TOKENS_CLIP, WIDTH), 1.0, 6.0, ((0, 16), (1, 32)))
    upstream = draw_upstream(jax.random.fold_in(keys[8], 71), 0)
    norm_gains = draw_norm_gains(jax.random.fold_in(keys[8], 71), 0)
    return dict(q_spatial=q_spatial, k_spatial=k_spatial, v_spatial=v_spatial, q_temporal=q_temporal, k_temporal=k_temporal, v_temporal=v_temporal, upstream=upstream, norm_gains=norm_gains)


EPS = 1e-06

def norm_rows(raw, gain):
    full = raw.astype(jnp.float32)
    inv = lax.rsqrt(lax.optimization_barrier(jnp.mean(full * full, axis=-1, keepdims=True)) + EPS)
    return ((full * inv * gain).astype(jnp.bfloat16), inv)

def norm_back(raw, inv, gain, grad):
    full = raw.astype(jnp.float32)
    scaled = gain * grad
    result = inv * scaled - full * inv ** 3 * lax.optimization_barrier(jnp.mean(full * scaled, axis=-1, keepdims=True))
    gain_term = lax.optimization_barrier(jnp.sum((grad * full * inv).reshape(-1, raw.shape[-1]), axis=0))
    return (result.astype(jnp.bfloat16), gain_term)

def attend_one(normed_query_rows, normed_key_rows, value_rows, output_gradient):
    softmax_scale = HEAD_DIM ** (-0.5)
    logit_matrix = jnp.einsum('axe,sxe->xas', normed_query_rows.astype(jnp.float32), normed_key_rows.astype(jnp.float32)) * softmax_scale
    probs = jax.nn.softmax(logit_matrix, axis=-1)
    softmax_weights = probs.astype(jnp.bfloat16)
    probs_gradient = jnp.einsum('axe,sxe->xas', output_gradient.astype(jnp.float32), value_rows.astype(jnp.float32))
    delta = lax.optimization_barrier(jnp.sum(probs * probs_gradient, axis=-1, keepdims=True))
    scores_gradient = (probs * (probs_gradient - delta) * softmax_scale).astype(jnp.bfloat16)
    normed_query_gradient = jnp.einsum('fjz,zfc->jfc', scores_gradient.astype(jnp.float32), normed_key_rows.astype(jnp.float32))
    normed_key_gradient = jnp.einsum('roy,orj->yrj', scores_gradient.astype(jnp.float32), normed_query_rows.astype(jnp.float32))
    value_gradient = jnp.einsum('roy,orj->yrj', softmax_weights.astype(jnp.float32), output_gradient.astype(jnp.float32))
    return (normed_query_gradient, normed_key_gradient, value_gradient.astype(jnp.bfloat16))

def reference(q_spatial, k_spatial, v_spatial, q_temporal, k_temporal, v_temporal, upstream, norm_gains):
    shape = (CLIPS, FRAMES, S_FRAME, HEADS, HEAD_DIM)
    spatial_shape = (CLIPS * FRAMES, S_FRAME, HEADS, HEAD_DIM)
    qs = q_spatial.reshape(shape)
    ks = k_spatial.reshape(shape)
    qt = q_temporal.reshape(shape)
    kt = k_temporal.reshape(shape)
    output_gradient = upstream.reshape(shape)
    spatial_normed_queries, qs_inv = norm_rows(qs, norm_gains[0])
    spatial_normed_keys, ks_inv = norm_rows(ks, norm_gains[1])
    qt_n, qt_inv = norm_rows(qt, norm_gains[2])
    kt_n, kt_inv = norm_rows(kt, norm_gains[3])

    def spatial_one(items):
        return attend_one(items[0], items[1], items[2], items[3])
    dqs, dks, dvs = lax.map(spatial_one, (spatial_normed_queries.reshape(spatial_shape), spatial_normed_keys.reshape(spatial_shape), v_spatial.reshape(spatial_shape), output_gradient.reshape(spatial_shape)))

    def to_pos(arr):
        return jnp.transpose(arr, (0, 2, 1, 3, 4)).reshape(CLIPS * S_FRAME, FRAMES, HEADS, HEAD_DIM)

    def from_pos(arr):
        return jnp.transpose(arr.reshape(CLIPS, S_FRAME, FRAMES, HEADS, HEAD_DIM), (0, 2, 1, 3, 4))
    dqt, dkt, dvt = jax.vmap(attend_one)(to_pos(qt_n), to_pos(kt_n), to_pos(v_temporal.reshape(shape)), to_pos(output_gradient))
    grad_qs, gain_qs = norm_back(qs, qs_inv, norm_gains[0], dqs.reshape(shape))
    grad_ks, gain_ks = norm_back(ks, ks_inv, norm_gains[1], dks.reshape(shape))
    grad_qt, gain_qt = norm_back(qt, qt_inv, norm_gains[2], from_pos(dqt))
    grad_kt, gain_kt = norm_back(kt, kt_inv, norm_gains[3], from_pos(dkt))
    count = float(CLIPS * TOKENS_CLIP * HEADS)
    gains = jnp.stack([gain_qs, gain_ks, gain_qt, gain_kt], 0) / jnp.sqrt(jnp.float32(count))
    flat = (CLIPS, TOKENS_CLIP, WIDTH)
    return (grad_qs.reshape(flat), grad_ks.reshape(flat), dvs.reshape(flat), grad_qt.reshape(flat), grad_kt.reshape(flat), from_pos(dvt).reshape(flat), gains)
```

```python
import functools
import math

import jax
import jax.numpy as jnp
from jax import lax
from jax.experimental import pallas as pl
from jax.experimental.pallas import tpu as pltpu
from jax.sharding import PartitionSpec as P

D = 128
FRAMES = 4
EPS = 1e-06
SCALE = D**-0.5
F32, BF16 = jnp.float32, jnp.bfloat16
CHIPS = 4
QBLK = 256

VMEM = pl.BlockSpec(memory_space=pltpu.VMEM)
SMEM = pl.BlockSpec(memory_space=pltpu.SMEM)


def params(mib=48):
    return pltpu.CompilerParams(vmem_limit_bytes=mib * 2**20)


def dot(a, b):
    return jnp.dot(a, b, preferred_element_type=F32)


def dot_t(a, b):
    return lax.dot_general(a, b, (((1,), (1,)), ((), ())), preferred_element_type=F32)


def inv_of(raw):
    full = raw.astype(F32)
    return lax.rsqrt(jnp.mean(full * full, axis=-1, keepdims=True) + EPS)


def norm_back(raw, inv, gain, grad):
    full = raw.astype(F32)
    scaled = gain * grad
    result = inv * scaled - full * (inv * inv * inv) * jnp.mean(full * scaled, axis=-1, keepdims=True)
    gain_term = jnp.sum(grad * full * inv, axis=0, keepdims=True)
    return result.astype(BF16), gain_term


def cols(head):
    return slice(head * D, (head + 1) * D)


def spatial_pack_kernel(q, k, v, g, out):
    for c in range(CHIPS):
        a, b, e = cols(3 * c), cols(3 * c + 1), cols(3 * c + 2)
        for i, (ref, h) in enumerate([(q, a), (k, a), (v, a), (g, a), (q, b), (g, b)]):
            out[2 * c, i] = ref[:, h]
        for i, (ref, h) in enumerate([(q, e), (k, e), (v, e), (g, e), (k, b), (v, b)]):
            out[2 * c + 1, i] = ref[:, h]


def spatial_kernel(core_ref, gains, mine, other, out, gain_out, qn, kn, knt, gg, vv, raw_q, raw_k, dq, dk, dv):
    core = core_ref[0]
    n = qn.shape[0]
    srcs = mine.shape[0]
    tok = n // srcs
    gain_q, gain_k = gains[0:1, :], gains[1:2, :]

    def flat(x):
        return x.reshape(n, D)

    def head():
        q, k = raw_q[...], raw_k[...]
        inv_q, inv_k = inv_of(q), inv_of(k)
        qn[...] = (q.astype(F32) * inv_q * gain_q).astype(BF16)
        k_n = (k.astype(F32) * inv_k * gain_k).astype(BF16)
        kn[...] = k_n
        knt[...] = k_n.astype(F32).T.astype(BF16)
        dk[...] = jnp.zeros_like(dk)
        dv[...] = jnp.zeros_like(dv)

        def step(i, carry):
            rows = pl.ds(pl.multiple_of(i * QBLK, QBLK), QBLK)
            qb, gb = qn[rows, :], gg[rows, :]
            s = dot_t(kn[...], qb) * SCALE
            e = jnp.exp(s - jnp.max(s, axis=0, keepdims=True))
            p = e * (1.0 / jnp.sum(e, axis=0, keepdims=True))
            dp = dot_t(vv[...], gb)
            delta = jnp.sum(p * dp, axis=0, keepdims=True)
            ds = (p * (dp - delta) * SCALE).astype(BF16)
            dv[...] += dot(p.astype(BF16), gb)
            dk[...] += dot(ds, qb)
            dq[rows, :] = dot(knt[...], ds).T
            return carry

        lax.fori_loop(0, n // QBLK, step, 0)
        grad_q, term_q = norm_back(q, inv_q, gain_q, dq[...])
        grad_k, term_k = norm_back(k, inv_k, gain_k, dk[...])
        return grad_q, grad_k, dv[...].astype(BF16), term_q, term_k

    def blocks(x):
        return x.reshape(srcs, tok, D)

    raw_q[...] = flat(mine[:, 0])
    raw_k[...] = flat(mine[:, 1])
    vv[...] = flat(mine[:, 2])
    gg[...] = flat(mine[:, 3])
    grad_q, grad_k, grad_v, term_q, term_k = head()
    out[:, 0:tok] = blocks(grad_q)
    out[:, tok : 2 * tok] = blocks(grad_k)
    out[:, 2 * tok : 3 * tok] = blocks(grad_v)
    gain_out[...] = jnp.zeros_like(gain_out)
    gain_out[0:1, :] = term_q
    gain_out[1:2, :] = term_k

    @pl.when(core == 0)
    def _():
        raw_q[...] = flat(mine[:, 4])
        gg[...] = flat(mine[:, 5])
        raw_k[...] = flat(other[:, 0])
        vv[...] = flat(other[:, 1])

    @pl.when(core == 1)
    def _():
        raw_k[...] = flat(mine[:, 4])
        vv[...] = flat(mine[:, 5])
        raw_q[...] = flat(other[:, 0])
        gg[...] = flat(other[:, 1])

    grad_q, grad_k, grad_v, term_q, term_k = head()
    half = tok // 2

    @pl.when(core == 0)
    def _():
        out[:, 3 * tok : 4 * tok] = blocks(grad_q)
        out[:, 4 * tok : 4 * tok + half] = blocks(grad_v)[:, :half]
        gain_out[0:1, :] += term_q

    @pl.when(core == 1)
    def _():
        out[:, 3 * tok : 4 * tok] = blocks(grad_k)
        out[:, 4 * tok : 4 * tok + half] = blocks(grad_v)[:, half:]
        gain_out[1:2, :] += term_k


def spatial_unpack_kernel(got, grad_q, grad_k, grad_v):
    tok = grad_q.shape[0]
    half = tok // 2
    for c in range(CHIPS):
        a, b, e = cols(3 * c), cols(3 * c + 1), cols(3 * c + 2)
        for core, h in ((0, a), (1, e)):
            src = 2 * c + core
            grad_q[:, h] = got[src, 0:tok]
            grad_k[:, h] = got[src, tok : 2 * tok]
            grad_v[:, h] = got[src, 2 * tok : 3 * tok]
        grad_q[:, b] = got[2 * c, 3 * tok : 4 * tok]
        grad_k[:, b] = got[2 * c + 1, 3 * tok : 4 * tok]
        grad_v[0:half, b] = got[2 * c, 4 * tok : 4 * tok + half]
        grad_v[half:tok, b] = got[2 * c + 1, 4 * tok : 4 * tok + half]


def temporal_kernel(gains, got, out, gain_out):
    frames, _, pos, width = got.shape
    n = frames * pos
    gain_q, gain_k = gains[2:3, :], gains[3:4, :]
    row = lax.broadcasted_iota(jnp.int32, (n, n), 0)
    col = lax.broadcasted_iota(jnp.int32, (n, n), 1)
    same = lax.rem(row, pos) == lax.rem(col, pos)
    sum_q, sum_k = jnp.zeros((1, D), F32), jnp.zeros((1, D), F32)
    for h in range(width // D):
        q, k, v, g = (got[:, i, :, cols(h)].reshape(n, D) for i in range(4))
        inv_q, inv_k = inv_of(q), inv_of(k)
        q_n = (q.astype(F32) * inv_q * gain_q).astype(BF16)
        k_n = (k.astype(F32) * inv_k * gain_k).astype(BF16)
        s = jnp.where(same, dot_t(k_n, q_n) * SCALE, -1e30)
        e = jnp.exp(s - jnp.max(s, axis=0, keepdims=True))
        p = e * (1.0 / jnp.sum(e, axis=0, keepdims=True))
        dp = dot_t(v, g)
        delta = jnp.sum(p * dp, axis=0, keepdims=True)
        ds = (p * (dp - delta) * SCALE).astype(BF16)
        dv = dot(p.astype(BF16), g)
        dk = dot(ds, q_n)
        dq = dot(ds.astype(F32).T.astype(BF16), k_n)
        grad_q, term_q = norm_back(q, inv_q, gain_q, dq)
        grad_k, term_k = norm_back(k, inv_k, gain_k, dk)
        sum_q += term_q
        sum_k += term_k
        for i, x in enumerate((grad_q, grad_k, dv.astype(BF16))):
            out[:, i, :, cols(h)] = x.reshape(frames, pos, D)
    gain_out[...] = jnp.zeros_like(gain_out)
    gain_out[2:3, :] = sum_q
    gain_out[3:4, :] = sum_k


def swap(x, axis, bit):
    count = lax.axis_size(axis)
    return lax.ppermute(x, axis, [(i, i ^ bit) for i in range(count)])


def sum_all(x):
    for axis in ("seq", "dp"):
        bit = 1
        while bit < lax.axis_size(axis):
            x = x + swap(x, axis, bit)
            bit *= 2
    return x


def local(q_spatial, k_spatial, v_spatial, q_temporal, k_temporal, v_temporal, upstream, norm_gains):
    tok, width = q_spatial.shape[1:]
    nseq = lax.axis_size("seq")
    group = nseq // FRAMES
    frame_groups = [[f * group + j for j in range(group)] for f in range(FRAMES)]
    place_groups = [[f * group + j for f in range(FRAMES)] for j in range(group)]
    core = (lax.axis_index("seq") & 1).astype(jnp.int32).reshape(1)

    packed = pl.pallas_call(
        spatial_pack_kernel,
        out_shape=jax.ShapeDtypeStruct((group, 6, tok, D), BF16),
        in_specs=[VMEM] * 4,
        out_specs=VMEM,
        compiler_params=params(),
        name="spatial_pack",
    )(q_spatial[0], k_spatial[0], v_spatial[0], upstream[0])
    mine = lax.all_to_all(
        packed.reshape(group, 6 * tok, D), "seq", 0, 0, axis_index_groups=frame_groups, tiled=True
    ).reshape(group, 6, tok, D)

    pos = tok // FRAMES
    shares = jnp.stack(
        [x[0].reshape(FRAMES, pos, width) for x in (q_temporal, k_temporal, v_temporal, upstream)], 1
    ).reshape(FRAMES, 4 * pos, width)
    mine, shares = lax.optimization_barrier((mine, shares))
    got = lax.all_to_all(shares, "seq", 0, 0, axis_index_groups=place_groups, tiled=True)

    other = swap(mine[:, 4:6], "seq", 1)
    n = group * tok
    spatial_grads, spatial_terms = pl.pallas_call(
        spatial_kernel,
        out_shape=(
            jax.ShapeDtypeStruct((group, 4 * tok + tok // 2, D), BF16),
            jax.ShapeDtypeStruct((8, D), F32),
        ),
        in_specs=[SMEM, VMEM, VMEM, VMEM],
        out_specs=(VMEM, VMEM),
        scratch_shapes=[
            pltpu.VMEM((n, D), BF16),
            pltpu.VMEM((n, D), BF16),
            pltpu.VMEM((D, n), BF16),
            pltpu.VMEM((n, D), BF16),
            pltpu.VMEM((n, D), BF16),
            pltpu.VMEM((n, D), BF16),
            pltpu.VMEM((n, D), BF16),
            pltpu.VMEM((n, D), F32),
            pltpu.VMEM((n, D), F32),
            pltpu.VMEM((n, D), F32),
        ],
        compiler_params=params(),
        cost_estimate=pl.CostEstimate(
            flops=20 * n * n * D, bytes_accessed=30 * n * D, transcendentals=2 * n * n
        ),
        name="spatial_backward",
    )(core, norm_gains, mine, other)
    spatial_back = lax.all_to_all(
        spatial_grads, "seq", 0, 0, axis_index_groups=frame_groups, tiled=True
    )

    temporal_grads, temporal_terms = pl.pallas_call(
        temporal_kernel,
        out_shape=(
            jax.ShapeDtypeStruct((FRAMES, 3, pos, width), BF16),
            jax.ShapeDtypeStruct((8, D), F32),
        ),
        in_specs=[VMEM, VMEM],
        out_specs=(VMEM, VMEM),
        compiler_params=params(),
        cost_estimate=pl.CostEstimate(
            flops=10 * tok * tok * width, bytes_accessed=14 * tok * width, transcendentals=tok * tok * 12
        ),
        name="temporal_backward",
    )(norm_gains, got.reshape(FRAMES, 4, pos, width))
    temporal_back = lax.all_to_all(
        temporal_grads.reshape(FRAMES, 3 * pos, width), "seq", 0, 0, axis_index_groups=place_groups, tiled=True
    ).reshape(FRAMES, 3, pos, width)

    gains = sum_all(spatial_terms + temporal_terms)[:4]
    count = lax.axis_size("dp") * nseq * tok * (width // D)
    gains = gains / jnp.float32(math.sqrt(count))

    shape = jax.ShapeDtypeStruct((tok, width), BF16)
    grad_qs, grad_ks, grad_vs = pl.pallas_call(
        spatial_unpack_kernel,
        out_shape=(shape,) * 3,
        in_specs=[VMEM],
        out_specs=(VMEM,) * 3,
        compiler_params=params(),
        name="spatial_unpack",
    )(spatial_back)
    grad_qt, grad_kt, grad_vt = (temporal_back[:, i].reshape(1, tok, width) for i in range(3))
    return (grad_qs[None], grad_ks[None], grad_vs[None], grad_qt, grad_kt, grad_vt, gains)


def solution(mesh):
    rows = P("dp", "seq", None)
    return jax.shard_map(
        local, mesh=mesh, in_specs=(rows,) * 7 + (P(),), out_specs=(rows,) * 6 + (P(),), check_vma=False
    )
```

```python
import functools
import math

import jax
import jax.numpy as jnp
from jax import lax
from jax.experimental import pallas as pl
from jax.experimental.pallas import tpu as pltpu
from jax.sharding import PartitionSpec as P

D = 128
FRAMES = 4
EPS = 1e-06
SCALE = D**-0.5
F32, BF16 = jnp.float32, jnp.bfloat16
CHIPS = 4
QBLK = 256

VMEM = pl.BlockSpec(memory_space=pltpu.VMEM)
SMEM = pl.BlockSpec(memory_space=pltpu.SMEM)
HBM = pl.BlockSpec(memory_space=pltpu.HBM)


def params(mib=32):
    return pltpu.CompilerParams(vmem_limit_bytes=mib * 2**20)


def dot(a, b):
    return jnp.dot(a, b, preferred_element_type=F32)


def dot_t(a, b):
    return lax.dot_general(a, b, (((1,), (1,)), ((), ())), preferred_element_type=F32)


def inv_of(raw):
    full = raw.astype(F32)
    return lax.rsqrt(jnp.mean(full * full, axis=-1, keepdims=True) + EPS)


def norm_back(raw, inv, gain, grad):
    full = raw.astype(F32)
    scaled = gain * grad
    result = inv * scaled - full * (inv * inv * inv) * jnp.mean(full * scaled, axis=-1, keepdims=True)
    gain_term = jnp.sum(grad * full * inv, axis=0, keepdims=True)
    return result.astype(BF16), gain_term


def cols(head):
    return slice(head * D, (head + 1) * D)


def move(plan, name, outs, scalars, *operands, src=VMEM, dst=VMEM):
    n_in = len(operands)
    inside = src is VMEM and dst is VMEM
    count = len(plan(scalars, [Shape(x) for x in operands], [Shape(x) for x in outs]))

    def kernel(ids, *refs):
        outs_at = n_in + len(outs)
        pairs = plan([ids[i] for i in range(ids.shape[0])], refs[:n_in], refs[n_in:outs_at])
        if inside:
            for a, b in pairs:
                b[...] = a[...]
            return
        copies = [pltpu.make_async_copy(a, b, refs[-1].at[i]) for i, (a, b) in enumerate(pairs)]
        for c in copies:
            c.start()
        for c in copies:
            c.wait()

    return pl.pallas_call(
        kernel,
        out_shape=tuple(outs),
        in_specs=[SMEM] + [src] * n_in,
        out_specs=(dst,) * len(outs),
        scratch_shapes=[] if inside else [pltpu.SemaphoreType.DMA((count,))],
        compiler_params=params(16),
        cost_estimate=pl.CostEstimate(flops=0, bytes_accessed=0, transcendentals=0),
        name=name,
    )(jnp.stack(scalars), *operands)


class Shape:
    def __init__(self, x):
        self.shape = x.shape

    @property
    def at(self):
        return self

    def __getitem__(self, _):
        return self


def quarter(which, pos):
    return pl.ds(pl.multiple_of(which * pos, pos), pos)


def temporal_pack(ids, ins, outs):
    (frame,) = ids
    keep, to_x, to_z = outs
    pos = keep.shape[1]
    places = ((keep, 0), (to_x.at[0], 2), (to_x.at[1], 3), (to_z, 1))
    return [
        (x.at[quarter(frame ^ d, pos)], target.at[i])
        for target, d in places
        for i, x in enumerate(ins)
    ]


def forward_pack(ids, ins, outs):
    mine, from_x = ins
    return [(mine, outs[0].at[0]), (from_x.at[1], outs[0].at[1])]


def temporal_unpack(ids, ins, outs):
    (frame,) = ids
    pos = ins[0].shape[1]
    return [
        (r.at[i], x.at[quarter(frame ^ d, pos)])
        for d, r in enumerate(ins)
        for i, x in enumerate(outs)
    ]


def spatial_pack_kernel(q, k, v, g, out):
    for c in range(CHIPS):
        a, b, e = cols(3 * c), cols(3 * c + 1), cols(3 * c + 2)
        for i, (ref, h) in enumerate([(q, a), (k, a), (v, a), (g, a), (q, b), (g, b)]):
            out[2 * c, i] = ref[:, h]
        for i, (ref, h) in enumerate([(q, e), (k, e), (v, e), (g, e), (k, b), (v, b)]):
            out[2 * c + 1, i] = ref[:, h]


def spatial_kernel(core_ref, gains, mine, other, out, gain_out, qn, kn, knt, gg, vv, raw_q, raw_k, dq, dk, dv):
    core = core_ref[0]
    n = qn.shape[0]
    srcs = mine.shape[0]
    tok = n // srcs
    gain_q, gain_k = gains[0:1, :], gains[1:2, :]

    def flat(x):
        return x.reshape(n, D)

    def head():
        q, k = raw_q[...], raw_k[...]
        inv_q, inv_k = inv_of(q), inv_of(k)
        qn[...] = (q.astype(F32) * inv_q * gain_q).astype(BF16)
        k_n = (k.astype(F32) * inv_k * gain_k).astype(BF16)
        kn[...] = k_n
        knt[...] = k_n.astype(F32).T.astype(BF16)
        dk[...] = jnp.zeros_like(dk)
        dv[...] = jnp.zeros_like(dv)

        def step(i, carry):
            rows = pl.ds(pl.multiple_of(i * QBLK, QBLK), QBLK)
            qb, gb = qn[rows, :], gg[rows, :]
            s = dot_t(kn[...], qb) * SCALE
            e = jnp.exp(s - jnp.max(s, axis=0, keepdims=True))
            p = e * (1.0 / jnp.sum(e, axis=0, keepdims=True))
            dp = dot_t(vv[...], gb)
            delta = jnp.sum(p * dp, axis=0, keepdims=True)
            ds = (p * (dp - delta) * SCALE).astype(BF16)
            dv[...] += dot(p.astype(BF16), gb)
            dk[...] += dot(ds, qb)
            dq[rows, :] = dot(knt[...], ds).T
            return carry

        lax.fori_loop(0, n // QBLK, step, 0)
        grad_q, term_q = norm_back(q, inv_q, gain_q, dq[...])
        grad_k, term_k = norm_back(k, inv_k, gain_k, dk[...])
        return grad_q, grad_k, dv[...].astype(BF16), term_q, term_k

    def blocks(x):
        return x.reshape(srcs, tok, D)

    raw_q[...] = flat(mine[:, 0])
    raw_k[...] = flat(mine[:, 1])
    vv[...] = flat(mine[:, 2])
    gg[...] = flat(mine[:, 3])
    grad_q, grad_k, grad_v, term_q, term_k = head()
    out[:, 0:tok] = blocks(grad_q)
    out[:, tok : 2 * tok] = blocks(grad_k)
    out[:, 2 * tok : 3 * tok] = blocks(grad_v)
    gain_out[...] = jnp.zeros_like(gain_out)
    gain_out[0:1, :] = term_q
    gain_out[1:2, :] = term_k

    @pl.when(core == 0)
    def _():
        raw_q[...] = flat(mine[:, 4])
        gg[...] = flat(mine[:, 5])
        raw_k[...] = flat(other[:, 0])
        vv[...] = flat(other[:, 1])

    @pl.when(core == 1)
    def _():
        raw_k[...] = flat(mine[:, 4])
        vv[...] = flat(mine[:, 5])
        raw_q[...] = flat(other[:, 0])
        gg[...] = flat(other[:, 1])

    grad_q, grad_k, grad_v, term_q, term_k = head()
    half = tok // 2

    @pl.when(core == 0)
    def _():
        out[:, 3 * tok : 4 * tok] = blocks(grad_q)
        out[:, 4 * tok : 4 * tok + half] = blocks(grad_v)[:, :half]
        gain_out[0:1, :] += term_q

    @pl.when(core == 1)
    def _():
        out[:, 3 * tok : 4 * tok] = blocks(grad_k)
        out[:, 4 * tok : 4 * tok + half] = blocks(grad_v)[:, half:]
        gain_out[1:2, :] += term_k


def spatial_unpack_kernel(got, grad_q, grad_k, grad_v):
    tok = grad_q.shape[0]
    half = tok // 2
    for c in range(CHIPS):
        a, b, e = cols(3 * c), cols(3 * c + 1), cols(3 * c + 2)
        for core, h in ((0, a), (1, e)):
            src = 2 * c + core
            grad_q[:, h] = got[src, 0:tok]
            grad_k[:, h] = got[src, tok : 2 * tok]
            grad_v[:, h] = got[src, 2 * tok : 3 * tok]
        grad_q[:, b] = got[2 * c, 3 * tok : 4 * tok]
        grad_k[:, b] = got[2 * c + 1, 3 * tok : 4 * tok]
        grad_v[0:half, b] = got[2 * c, 4 * tok : 4 * tok + half]
        grad_v[half:tok, b] = got[2 * c + 1, 4 * tok : 4 * tok + half]


def temporal_kernel(gains, spatial_terms, own, from_x, from_z, own_out, out1, out2, out3, gain_out):
    ins = (own, from_z.at[0], from_x.at[0], from_z.at[1])
    outs = (own_out, out1, out2, out3)
    _, pos, width = own.shape
    n = FRAMES * pos
    gain_q, gain_k = gains[2:3, :], gains[3:4, :]
    row = lax.broadcasted_iota(jnp.int32, (n, n), 0)
    col = lax.broadcasted_iota(jnp.int32, (n, n), 1)
    same = lax.rem(row, pos) == lax.rem(col, pos)
    sum_q, sum_k = jnp.zeros((1, D), F32), jnp.zeros((1, D), F32)
    for h in range(width // D):
        at = slice(h * D, (h + 1) * D)
        q, k, v, g = (jnp.concatenate([x[i, :, at] for x in ins], axis=0) for i in range(4))
        inv_q, inv_k = inv_of(q), inv_of(k)
        q_n = (q.astype(F32) * inv_q * gain_q).astype(BF16)
        k_n = (k.astype(F32) * inv_k * gain_k).astype(BF16)
        s = jnp.where(same, dot_t(k_n, q_n) * SCALE, -1e30)
        e = jnp.exp(s - jnp.max(s, axis=0, keepdims=True))
        p = e * (1.0 / jnp.sum(e, axis=0, keepdims=True))
        dp = dot_t(v, g)
        delta = jnp.sum(p * dp, axis=0, keepdims=True)
        ds = (p * (dp - delta) * SCALE).astype(BF16)
        dv = dot(p.astype(BF16), g)
        dk = dot(ds, q_n)
        dq = dot(ds.astype(F32).T.astype(BF16), k_n)
        grad_q, term_q = norm_back(q, inv_q, gain_q, dq)
        grad_k, term_k = norm_back(k, inv_k, gain_k, dk)
        sum_q += term_q
        sum_k += term_k
        for i, x in enumerate((grad_q, grad_k, dv.astype(BF16))):
            for d, out in enumerate(outs):
                out[i, :, at] = x[d * pos : (d + 1) * pos]
    gain_out[...] = spatial_terms[...]
    gain_out[2:3, :] = sum_q
    gain_out[3:4, :] = sum_k


def swap(x, bits, axis="seq"):
    return lax.ppermute(x, axis, [(i, i ^ bits) for i in range(lax.axis_size(axis))])


def sum_over_z(x, groups):
    all_of = jnp.broadcast_to(x[None], (len(groups[0]), *x.shape))
    return jnp.sum(lax.all_to_all(all_of, "seq", 0, 0, axis_index_groups=groups, tiled=True), axis=0)


def local(q_spatial, k_spatial, v_spatial, q_temporal, k_temporal, v_temporal, upstream, norm_gains):
    tok, width = q_spatial.shape[1:]
    nseq = lax.axis_size("seq")
    group = nseq // FRAMES
    n = group * tok
    pos = tok // FRAMES
    at = lax.axis_index("seq").astype(jnp.int32)
    core, frame = at & 1, at // group
    frame_groups = [[f * group + j for j in range(group)] for f in range(FRAMES)]

    def shape(*dims):
        return jax.ShapeDtypeStruct(dims, BF16)

    def exchange(x):
        return lax.all_to_all(x, "seq", 0, 0, axis_index_groups=frame_groups, tiled=True)

    packed = pl.pallas_call(
        spatial_pack_kernel,
        out_shape=shape(group, 6, tok, D),
        in_specs=[VMEM] * 4,
        out_specs=VMEM,
        compiler_params=params(16),
        name="spatial_pack",
    )(q_spatial[0], k_spatial[0], v_spatial[0], upstream[0])
    mine = exchange(packed.reshape(group, 6 * tok, D)).reshape(group, 6, tok, D)
    keep, to_x, to_z = move(
        temporal_pack, "temporal_pack",
        [shape(4, pos, width), shape(2, 4, pos, width), shape(4, pos, width)], [frame],
        q_temporal[0], k_temporal[0], v_temporal[0], upstream[0], src=HBM,
    )
    from_x = swap(to_x, 2 * group)
    (to_z,) = move(forward_pack, "forward_pack", [shape(2, 4, pos, width)], [frame], to_z, from_x)
    mine, to_z = lax.optimization_barrier((mine, to_z))
    from_z = swap(to_z, group)

    other = swap(mine[:, 4:6], 1)
    spatial_grads, spatial_terms = pl.pallas_call(
        spatial_kernel,
        out_shape=(shape(group, 4 * tok + tok // 2, D), jax.ShapeDtypeStruct((8, D), F32)),
        in_specs=[SMEM, VMEM, VMEM, VMEM],
        out_specs=(VMEM, VMEM),
        scratch_shapes=[
            pltpu.VMEM((n, D), BF16),
            pltpu.VMEM((n, D), BF16),
            pltpu.VMEM((D, n), BF16),
            pltpu.VMEM((n, D), BF16),
            pltpu.VMEM((n, D), BF16),
            pltpu.VMEM((n, D), BF16),
            pltpu.VMEM((n, D), BF16),
            pltpu.VMEM((n, D), F32),
            pltpu.VMEM((n, D), F32),
            pltpu.VMEM((n, D), F32),
        ],
        compiler_params=params(),
        cost_estimate=pl.CostEstimate(flops=0, bytes_accessed=0, transcendentals=0),
        name="spatial_backward",
    )(core.reshape(1), norm_gains, mine, other)
    back = exchange(spatial_grads)

    piece = shape(3, pos, width)
    own, o1, o2, o3, terms = pl.pallas_call(
        temporal_kernel,
        out_shape=(piece,) * 4 + (jax.ShapeDtypeStruct((8, D), F32),),
        in_specs=[VMEM] * 5,
        out_specs=(VMEM,) * 5,
        compiler_params=params(),
        cost_estimate=pl.CostEstimate(
            flops=10000 * tok * tok * width, bytes_accessed=14 * tok * width, transcendentals=tok * tok * 12
        ),
        name="temporal_backward",
    )(norm_gains, spatial_terms, keep, from_x, from_z)
    b1, b2, b3 = swap(o1, group), swap(o2, 2 * group), swap(o3, 3 * group)
    for axis, bits in (("dp", 1), ("seq", nseq // 2), ("dp", 2), ("dp", 4), ("dp", 8), ("seq", 1)):
        terms = terms + swap(terms, bits, axis)
    terms, back, b1, b3 = lax.optimization_barrier((terms, back, b1, b3))
    z_groups = [[x * nseq // 2 + c + i for i in range(0, nseq // 2, 2)] for x in range(2) for c in range(2)]
    gains = sum_over_z(terms, z_groups)[:4]
    grad_qt, grad_kt, grad_vt = move(
        temporal_unpack, "temporal_unpack", [shape(tok, width)] * 3, [frame], own, b1, b2, b3, dst=HBM
    )
    grad_qs, grad_ks, grad_vs = pl.pallas_call(
        spatial_unpack_kernel,
        out_shape=(shape(tok, width),) * 3,
        in_specs=[VMEM],
        out_specs=(VMEM,) * 3,
        compiler_params=params(16),
        name="spatial_unpack",
    )(back)

    count = lax.axis_size("dp") * nseq * tok * (width // D)
    gains = gains / jnp.float32(math.sqrt(count))
    return (grad_qs[None], grad_ks[None], grad_vs[None], grad_qt[None], grad_kt[None], grad_vt[None], gains)


def solution(mesh):
    rows = P("dp", "seq", None)
    return jax.shard_map(
        local, mesh=mesh, in_specs=(rows,) * 7 + (P(),), out_specs=(rows,) * 6 + (P(),), check_vma=False
    )
```

```python
import functools
import math

import jax
import jax.numpy as jnp
from jax import lax
from jax.experimental import pallas as pl
from jax.experimental.pallas import tpu as pltpu
from jax.sharding import PartitionSpec as P

D = 128
FRAMES = 4
EPS = 1e-06
SCALE = D**-0.5
F32, BF16 = jnp.float32, jnp.bfloat16
CHIPS = 4
QBLK = 256

VMEM = pl.BlockSpec(memory_space=pltpu.VMEM)
SMEM = pl.BlockSpec(memory_space=pltpu.SMEM)
HBM = pl.BlockSpec(memory_space=pltpu.HBM)


def params(mib=32):
    return pltpu.CompilerParams(vmem_limit_bytes=mib * 2**20)


def dot(a, b):
    return jnp.dot(a, b, preferred_element_type=F32)


def dot_t(a, b):
    return lax.dot_general(a, b, (((1,), (1,)), ((), ())), preferred_element_type=F32)


def inv_of(raw):
    full = raw.astype(F32)
    return lax.rsqrt(jnp.mean(full * full, axis=-1, keepdims=True) + EPS)


def norm_back(raw, inv, gain, grad):
    full = raw.astype(F32)
    scaled = gain * grad
    result = inv * scaled - full * (inv * inv * inv) * jnp.mean(full * scaled, axis=-1, keepdims=True)
    gain_term = jnp.sum(grad * full * inv, axis=0, keepdims=True)
    return result.astype(BF16), gain_term


def cols(head):
    return slice(head * D, (head + 1) * D)


def move(plan, name, outs, scalars, *operands, src=VMEM, dst=VMEM):
    n_in = len(operands)
    inside = src is VMEM and dst is VMEM
    count = len(plan(scalars, [Shape(x) for x in operands], [Shape(x) for x in outs]))

    def kernel(ids, *refs):
        outs_at = n_in + len(outs)
        pairs = plan([ids[i] for i in range(ids.shape[0])], refs[:n_in], refs[n_in:outs_at])
        if inside:
            for a, b in pairs:
                b[...] = a[...]
            return
        copies = [pltpu.make_async_copy(a, b, refs[-1].at[i]) for i, (a, b) in enumerate(pairs)]
        for c in copies:
            c.start()
        for c in copies:
            c.wait()

    return pl.pallas_call(
        kernel,
        out_shape=tuple(outs),
        in_specs=[SMEM] + [src] * n_in,
        out_specs=(dst,) * len(outs),
        scratch_shapes=[] if inside else [pltpu.SemaphoreType.DMA((count,))],
        compiler_params=params(16),
        cost_estimate=pl.CostEstimate(flops=0, bytes_accessed=0, transcendentals=0),
        name=name,
    )(jnp.stack(scalars), *operands)


class Shape:
    def __init__(self, x):
        self.shape = x.shape

    @property
    def at(self):
        return self

    def __getitem__(self, _):
        return self


def quarter(which, pos):
    return pl.ds(pl.multiple_of(which * pos, pos), pos)


def temporal_pack(ids, ins, outs):
    (frame,) = ids
    keep, to_x, to_z = outs
    pos = keep.shape[1]
    places = ((keep, 0), (to_x.at[0], 2), (to_x.at[1], 3), (to_z, 1))
    return [
        (x.at[quarter(frame ^ d, pos)], target.at[i])
        for target, d in places
        for i, x in enumerate(ins)
    ]


def forward_pack(ids, ins, outs):
    mine, from_x = ins
    return [(mine, outs[0].at[0]), (from_x.at[1], outs[0].at[1])]


def temporal_unpack(ids, ins, outs):
    (frame,) = ids
    own, from_x, from_z = ins
    pos = own.shape[1]
    places = ((own, 0), (from_x.at[0], 2), (from_z.at[0], 1), (from_z.at[1], 3))
    return [
        (r.at[i], x.at[quarter(frame ^ d, pos)])
        for r, d in places
        for i, x in enumerate(outs)
    ]


def spatial_pack_kernel(q, k, v, g, out):
    for c in range(CHIPS):
        a, b, e = cols(3 * c), cols(3 * c + 1), cols(3 * c + 2)
        for i, (ref, h) in enumerate([(q, a), (k, a), (v, a), (g, a), (q, b), (g, b)]):
            out[2 * c, i] = ref[:, h]
        for i, (ref, h) in enumerate([(q, e), (k, e), (v, e), (g, e), (k, b), (v, b)]):
            out[2 * c + 1, i] = ref[:, h]


def spatial_kernel(core_ref, gains, mine, other, out, gain_out, qn, kn, knt, gg, vv, raw_q, raw_k, dq, dk, dv):
    core = core_ref[0]
    n = qn.shape[0]
    srcs = mine.shape[0]
    tok = n // srcs
    gain_q, gain_k = gains[0:1, :], gains[1:2, :]

    def flat(x):
        return x.reshape(n, D)

    def head():
        q, k = raw_q[...], raw_k[...]
        inv_q, inv_k = inv_of(q), inv_of(k)
        qn[...] = (q.astype(F32) * inv_q * gain_q).astype(BF16)
        k_n = (k.astype(F32) * inv_k * gain_k).astype(BF16)
        kn[...] = k_n
        knt[...] = k_n.astype(F32).T.astype(BF16)
        dk[...] = jnp.zeros_like(dk)
        dv[...] = jnp.zeros_like(dv)

        def step(i, carry):
            rows = pl.ds(pl.multiple_of(i * QBLK, QBLK), QBLK)
            qb, gb = qn[rows, :], gg[rows, :]
            s = dot_t(kn[...], qb) * SCALE
            e = jnp.exp(s - jnp.max(s, axis=0, keepdims=True))
            p = e * (1.0 / jnp.sum(e, axis=0, keepdims=True))
            dp = dot_t(vv[...], gb)
            delta = jnp.sum(p * dp, axis=0, keepdims=True)
            ds = (p * (dp - delta) * SCALE).astype(BF16)
            dv[...] += dot(p.astype(BF16), gb)
            dk[...] += dot(ds, qb)
            dq[rows, :] = dot(knt[...], ds).T
            return carry

        lax.fori_loop(0, n // QBLK, step, 0)
        grad_q, term_q = norm_back(q, inv_q, gain_q, dq[...])
        grad_k, term_k = norm_back(k, inv_k, gain_k, dk[...])
        return grad_q, grad_k, dv[...].astype(BF16), term_q, term_k

    def blocks(x):
        return x.reshape(srcs, tok, D)

    raw_q[...] = flat(mine[:, 0])
    raw_k[...] = flat(mine[:, 1])
    vv[...] = flat(mine[:, 2])
    gg[...] = flat(mine[:, 3])
    grad_q, grad_k, grad_v, term_q, term_k = head()
    out[:, 0:tok] = blocks(grad_q)
    out[:, tok : 2 * tok] = blocks(grad_k)
    out[:, 2 * tok : 3 * tok] = blocks(grad_v)
    gain_out[...] = jnp.zeros_like(gain_out)
    gain_out[0:1, :] = term_q
    gain_out[1:2, :] = term_k

    @pl.when(core == 0)
    def _():
        raw_q[...] = flat(mine[:, 4])
        gg[...] = flat(mine[:, 5])
        raw_k[...] = flat(other[:, 0])
        vv[...] = flat(other[:, 1])

    @pl.when(core == 1)
    def _():
        raw_k[...] = flat(mine[:, 4])
        vv[...] = flat(mine[:, 5])
        raw_q[...] = flat(other[:, 0])
        gg[...] = flat(other[:, 1])

    grad_q, grad_k, grad_v, term_q, term_k = head()
    half = tok // 2

    @pl.when(core == 0)
    def _():
        out[:, 3 * tok : 4 * tok] = blocks(grad_q)
        out[:, 4 * tok : 4 * tok + half] = blocks(grad_v)[:, :half]
        gain_out[0:1, :] += term_q

    @pl.when(core == 1)
    def _():
        out[:, 3 * tok : 4 * tok] = blocks(grad_k)
        out[:, 4 * tok : 4 * tok + half] = blocks(grad_v)[:, half:]
        gain_out[1:2, :] += term_k


def spatial_unpack_kernel(got, grad_q, grad_k, grad_v):
    tok = grad_q.shape[0]
    half = tok // 2
    for c in range(CHIPS):
        a, b, e = cols(3 * c), cols(3 * c + 1), cols(3 * c + 2)
        for core, h in ((0, a), (1, e)):
            src = 2 * c + core
            grad_q[:, h] = got[src, 0:tok]
            grad_k[:, h] = got[src, tok : 2 * tok]
            grad_v[:, h] = got[src, 2 * tok : 3 * tok]
        grad_q[:, b] = got[2 * c, 3 * tok : 4 * tok]
        grad_k[:, b] = got[2 * c + 1, 3 * tok : 4 * tok]
        grad_v[0:half, b] = got[2 * c, 4 * tok : 4 * tok + half]
        grad_v[half:tok, b] = got[2 * c + 1, 4 * tok : 4 * tok + half]


def temporal_kernel(gains, spatial_terms, own, from_x, from_z, own_out, to_x, to_z, gain_out):
    ins = (own, from_x.at[0], from_z.at[0], from_z.at[1])
    outs = (own_out, to_x.at[0], to_z, to_x.at[1])
    _, pos, width = own.shape
    n = FRAMES * pos
    gain_q, gain_k = gains[2:3, :], gains[3:4, :]
    row = lax.broadcasted_iota(jnp.int32, (n, n), 0)
    col = lax.broadcasted_iota(jnp.int32, (n, n), 1)
    same = lax.rem(row, pos) == lax.rem(col, pos)
    sum_q, sum_k = jnp.zeros((1, D), F32), jnp.zeros((1, D), F32)
    for h in range(width // D):
        at = slice(h * D, (h + 1) * D)
        q, k, v, g = (jnp.concatenate([x[i, :, at] for x in ins], axis=0) for i in range(4))
        inv_q, inv_k = inv_of(q), inv_of(k)
        q_n = (q.astype(F32) * inv_q * gain_q).astype(BF16)
        k_n = (k.astype(F32) * inv_k * gain_k).astype(BF16)
        s = jnp.where(same, dot_t(k_n, q_n) * SCALE, -1e30)
        e = jnp.exp(s - jnp.max(s, axis=0, keepdims=True))
        p = e * (1.0 / jnp.sum(e, axis=0, keepdims=True))
        dp = dot_t(v, g)
        delta = jnp.sum(p * dp, axis=0, keepdims=True)
        ds = (p * (dp - delta) * SCALE).astype(BF16)
        dv = dot(p.astype(BF16), g)
        dk = dot(ds, q_n)
        dq = dot(ds.astype(F32).T.astype(BF16), k_n)
        grad_q, term_q = norm_back(q, inv_q, gain_q, dq)
        grad_k, term_k = norm_back(k, inv_k, gain_k, dk)
        sum_q += term_q
        sum_k += term_k
        for i, x in enumerate((grad_q, grad_k, dv.astype(BF16))):
            for d, out in enumerate(outs):
                out[i, :, at] = x[d * pos : (d + 1) * pos]
    gain_out[...] = spatial_terms[...]
    gain_out[2:3, :] = sum_q
    gain_out[3:4, :] = sum_k


def swap(x, bits, axis="seq"):
    return lax.ppermute(x, axis, [(i, i ^ bits) for i in range(lax.axis_size(axis))])


def add_swapped(x, bits, axis):
    return x + swap(x, bits, axis)


def sum_over(x, axis):
    all_of = jnp.broadcast_to(x[None], (lax.axis_size(axis), *x.shape))
    return jnp.sum(lax.all_to_all(all_of, axis, 0, 0, tiled=True), axis=0)


def local(q_spatial, k_spatial, v_spatial, q_temporal, k_temporal, v_temporal, upstream, norm_gains):
    tok, width = q_spatial.shape[1:]
    nseq = lax.axis_size("seq")
    group = nseq // FRAMES
    n = group * tok
    pos = tok // FRAMES
    at = lax.axis_index("seq").astype(jnp.int32)
    core, frame = at & 1, at // group
    frame_groups = [[f * group + j for j in range(group)] for f in range(FRAMES)]

    def shape(*dims):
        return jax.ShapeDtypeStruct(dims, BF16)

    def exchange(x):
        return lax.all_to_all(x, "seq", 0, 0, axis_index_groups=frame_groups, tiled=True)

    packed = pl.pallas_call(
        spatial_pack_kernel,
        out_shape=shape(group, 6, tok, D),
        in_specs=[VMEM] * 4,
        out_specs=VMEM,
        compiler_params=params(16),
        name="spatial_pack",
    )(q_spatial[0], k_spatial[0], v_spatial[0], upstream[0])
    mine = exchange(packed.reshape(group, 6 * tok, D)).reshape(group, 6, tok, D)
    keep, to_x, to_z = move(
        temporal_pack, "temporal_pack",
        [shape(4, pos, width), shape(2, 4, pos, width), shape(4, pos, width)], [frame],
        q_temporal[0], k_temporal[0], v_temporal[0], upstream[0], src=HBM,
    )
    from_x = swap(to_x, 2 * group)
    (to_z,) = move(forward_pack, "forward_pack", [shape(2, 4, pos, width)], [frame], to_z, from_x)
    mine, to_z = lax.optimization_barrier((mine, to_z))
    from_z = swap(to_z, group)

    other = swap(mine[:, 4:6], 1)
    spatial_grads, spatial_terms = pl.pallas_call(
        spatial_kernel,
        out_shape=(shape(group, 4 * tok + tok // 2, D), jax.ShapeDtypeStruct((8, D), F32)),
        in_specs=[SMEM, VMEM, VMEM, VMEM],
        out_specs=(VMEM, VMEM),
        scratch_shapes=[
            pltpu.VMEM((n, D), BF16),
            pltpu.VMEM((n, D), BF16),
            pltpu.VMEM((D, n), BF16),
            pltpu.VMEM((n, D), BF16),
            pltpu.VMEM((n, D), BF16),
            pltpu.VMEM((n, D), BF16),
            pltpu.VMEM((n, D), BF16),
            pltpu.VMEM((n, D), F32),
            pltpu.VMEM((n, D), F32),
            pltpu.VMEM((n, D), F32),
        ],
        compiler_params=params(),
        cost_estimate=pl.CostEstimate(flops=0, bytes_accessed=0, transcendentals=0),
        name="spatial_backward",
    )(core.reshape(1), norm_gains, mine, other)
    back = exchange(spatial_grads)

    piece = shape(3, pos, width)
    own, to_x, to_z, terms = pl.pallas_call(
        temporal_kernel,
        out_shape=(piece, shape(2, 3, pos, width), piece, jax.ShapeDtypeStruct((8, D), F32)),
        in_specs=[VMEM] * 5,
        out_specs=(VMEM,) * 4,
        compiler_params=params(),
        cost_estimate=pl.CostEstimate(
            flops=10000 * tok * tok * width, bytes_accessed=14 * tok * width, transcendentals=tok * tok * 12
        ),
        name="temporal_backward",
    )(norm_gains, spatial_terms, keep, from_x, from_z)
    back_x = swap(to_x, 2 * group)
    terms = add_swapped(add_swapped(terms, 2, "dp"), 4, "dp")
    to_z, terms = lax.optimization_barrier((to_z, terms))
    (to_z,) = move(forward_pack, "forward_back_pack", [shape(2, 3, pos, width)], [frame], to_z, back_x)
    back_z = swap(to_z, group)
    terms = add_swapped(add_swapped(terms, 8, "dp"), 1, "dp")
    terms, back = lax.optimization_barrier((terms, back))
    gains = sum_over(terms, "seq")[:4]
    grad_qt, grad_kt, grad_vt = move(
        temporal_unpack, "temporal_unpack", [shape(tok, width)] * 3, [frame], own, back_x, back_z, dst=HBM
    )
    grad_qs, grad_ks, grad_vs = pl.pallas_call(
        spatial_unpack_kernel,
        out_shape=(shape(tok, width),) * 3,
        in_specs=[VMEM],
        out_specs=(VMEM,) * 3,
        compiler_params=params(16),
        name="spatial_unpack",
    )(back)

    count = lax.axis_size("dp") * nseq * tok * (width // D)
    gains = gains / jnp.float32(math.sqrt(count))
    return (grad_qs[None], grad_ks[None], grad_vs[None], grad_qt[None], grad_kt[None], grad_vt[None], gains)


def solution(mesh):
    rows = P("dp", "seq", None)
    return jax.shard_map(
        local, mesh=mesh, in_specs=(rows,) * 7 + (P(),), out_specs=(rows,) * 6 + (P(),), check_vma=False
    )
```

```python
import functools
import math

import jax
import jax.numpy as jnp
from jax import lax
from jax.experimental import pallas as pl
from jax.experimental.pallas import tpu as pltpu
from jax.sharding import PartitionSpec as P

D = 128
FRAMES = 4
EPS = 1e-06
SCALE = D**-0.5
F32, BF16 = jnp.float32, jnp.bfloat16
CHIPS = 4
QBLK = 256

VMEM = pl.BlockSpec(memory_space=pltpu.VMEM)
SMEM = pl.BlockSpec(memory_space=pltpu.SMEM)
HBM = pl.BlockSpec(memory_space=pltpu.HBM)


def params(mib=32):
    return pltpu.CompilerParams(vmem_limit_bytes=mib * 2**20)


def dot(a, b):
    return jnp.dot(a, b, preferred_element_type=F32)


def dot_t(a, b):
    return lax.dot_general(a, b, (((1,), (1,)), ((), ())), preferred_element_type=F32)


def inv_of(raw):
    full = raw.astype(F32)
    return lax.rsqrt(jnp.mean(full * full, axis=-1, keepdims=True) + EPS)


def norm_back(raw, inv, gain, grad):
    full = raw.astype(F32)
    scaled = gain * grad
    result = inv * scaled - full * (inv * inv * inv) * jnp.mean(full * scaled, axis=-1, keepdims=True)
    gain_term = jnp.sum(grad * full * inv, axis=0, keepdims=True)
    return result.astype(BF16), gain_term


def cols(head):
    return slice(head * D, (head + 1) * D)


def move(plan, name, outs, scalars, *operands, src=VMEM, dst=VMEM):
    n_in = len(operands)
    inside = src is VMEM and dst is VMEM
    count = len(plan(scalars, [Shape(x) for x in operands], [Shape(x) for x in outs]))

    def kernel(ids, *refs):
        outs_at = n_in + len(outs)
        pairs = plan([ids[i] for i in range(ids.shape[0])], refs[:n_in], refs[n_in:outs_at])
        if inside:
            for a, b in pairs:
                b[...] = a[...]
            return
        copies = [pltpu.make_async_copy(a, b, refs[-1].at[i]) for i, (a, b) in enumerate(pairs)]
        for c in copies:
            c.start()
        for c in copies:
            c.wait()

    return pl.pallas_call(
        kernel,
        out_shape=tuple(outs),
        in_specs=[SMEM] + [src] * n_in,
        out_specs=(dst,) * len(outs),
        scratch_shapes=[] if inside else [pltpu.SemaphoreType.DMA((count,))],
        compiler_params=params(16),
        cost_estimate=pl.CostEstimate(flops=0, bytes_accessed=0, transcendentals=0),
        name=name,
    )(jnp.stack(scalars), *operands)


class Shape:
    def __init__(self, x):
        self.shape = x.shape

    @property
    def at(self):
        return self

    def __getitem__(self, _):
        return self


def quarter(which, pos):
    return pl.ds(pl.multiple_of(which * pos, pos), pos)


def temporal_pack(ids, ins, outs):
    (frame,) = ids
    keep, to_x, to_z = outs
    pos = keep.shape[1]
    places = ((keep, 0), (to_x.at[0], 2), (to_x.at[1], 3), (to_z, 1))
    return [
        (x.at[quarter(frame ^ d, pos)], target.at[i])
        for target, d in places
        for i, x in enumerate(ins)
    ]


def forward_pack(ids, ins, outs):
    mine, from_x = ins
    return [(mine, outs[0].at[0]), (from_x.at[1], outs[0].at[1])]


def temporal_unpack(ids, ins, outs):
    (frame,) = ids
    own, from_x, from_z = ins
    pos = own.shape[1]
    places = ((own, 0), (from_x.at[0], 2), (from_z.at[0], 1), (from_z.at[1], 3))
    return [
        (r.at[i], x.at[quarter(frame ^ d, pos)])
        for r, d in places
        for i, x in enumerate(outs)
    ]


def spatial_pack_kernel(q, k, v, g, out, held, read, write):
    targets = []
    for c in range(CHIPS):
        a, b, e = cols(3 * c), cols(3 * c + 1), cols(3 * c + 2)
        targets.append([(q, a), (k, a), (v, a), (g, a), (q, b), (g, b)])
        targets.append([(q, e), (k, e), (v, e), (g, e), (k, b), (v, b)])
    blocks = [
        [pltpu.make_async_copy(x.at[:, h], held.at[t, i], read.at[t, i]) for i, (x, h) in enumerate(target)]
        for t, target in enumerate(targets)
    ]
    ends = [pltpu.make_async_copy(held.at[t], out.at[t], write.at[t]) for t in range(len(targets))]
    for target in blocks:
        for block in target:
            block.start()
    for target, end in zip(blocks, ends):
        for block in target:
            block.wait()
        end.start()
    for end in ends:
        end.wait()


def spatial_kernel(core_ref, gains, mine, other, out, gain_out, qn, kn, knt, gg, vv, raw_q, raw_k, dq, dk, dv):
    core = core_ref[0]
    n = qn.shape[0]
    srcs = mine.shape[0]
    tok = n // srcs
    gain_q, gain_k = gains[0:1, :], gains[1:2, :]

    def flat(x):
        return x.reshape(n, D)

    def head():
        q, k = raw_q[...], raw_k[...]
        inv_q, inv_k = inv_of(q), inv_of(k)
        qn[...] = (q.astype(F32) * inv_q * gain_q).astype(BF16)
        k_n = (k.astype(F32) * inv_k * gain_k).astype(BF16)
        kn[...] = k_n
        knt[...] = k_n.astype(F32).T.astype(BF16)
        dk[...] = jnp.zeros_like(dk)
        dv[...] = jnp.zeros_like(dv)

        def step(i, carry):
            rows = pl.ds(pl.multiple_of(i * QBLK, QBLK), QBLK)
            qb, gb = qn[rows, :], gg[rows, :]
            s = dot_t(kn[...], qb) * SCALE
            e = jnp.exp(s - jnp.max(s, axis=0, keepdims=True))
            p = e * (1.0 / jnp.sum(e, axis=0, keepdims=True))
            dp = dot_t(vv[...], gb)
            delta = jnp.sum(p * dp, axis=0, keepdims=True)
            ds = (p * (dp - delta) * SCALE).astype(BF16)
            dv[...] += dot(p.astype(BF16), gb)
            dk[...] += dot(ds, qb)
            dq[rows, :] = dot(knt[...], ds).T
            return carry

        lax.fori_loop(0, n // QBLK, step, 0)
        grad_q, term_q = norm_back(q, inv_q, gain_q, dq[...])
        grad_k, term_k = norm_back(k, inv_k, gain_k, dk[...])
        return grad_q, grad_k, dv[...].astype(BF16), term_q, term_k

    def blocks(x):
        return x.reshape(srcs, tok, D)

    raw_q[...] = flat(mine[:, 0])
    raw_k[...] = flat(mine[:, 1])
    vv[...] = flat(mine[:, 2])
    gg[...] = flat(mine[:, 3])
    grad_q, grad_k, grad_v, term_q, term_k = head()
    out[:, 0:tok] = blocks(grad_q)
    out[:, tok : 2 * tok] = blocks(grad_k)
    out[:, 2 * tok : 3 * tok] = blocks(grad_v)
    gain_out[...] = jnp.zeros_like(gain_out)
    gain_out[0:1, :] = term_q
    gain_out[1:2, :] = term_k

    @pl.when(core == 0)
    def _():
        raw_q[...] = flat(mine[:, 4])
        gg[...] = flat(mine[:, 5])
        raw_k[...] = flat(other[:, 0])
        vv[...] = flat(other[:, 1])

    @pl.when(core == 1)
    def _():
        raw_k[...] = flat(mine[:, 4])
        vv[...] = flat(mine[:, 5])
        raw_q[...] = flat(other[:, 0])
        gg[...] = flat(other[:, 1])

    grad_q, grad_k, grad_v, term_q, term_k = head()
    half = tok // 2

    @pl.when(core == 0)
    def _():
        out[:, 3 * tok : 4 * tok] = blocks(grad_q)
        out[:, 4 * tok : 4 * tok + half] = blocks(grad_v)[:, :half]
        gain_out[0:1, :] += term_q

    @pl.when(core == 1)
    def _():
        out[:, 3 * tok : 4 * tok] = blocks(grad_k)
        out[:, 4 * tok : 4 * tok + half] = blocks(grad_v)[:, half:]
        gain_out[1:2, :] += term_k


def spatial_unpack_kernel(got, grad_q, grad_k, grad_v):
    tok = grad_q.shape[0]
    half = tok // 2
    for c in range(CHIPS):
        a, b, e = cols(3 * c), cols(3 * c + 1), cols(3 * c + 2)
        for core, h in ((0, a), (1, e)):
            src = 2 * c + core
            grad_q[:, h] = got[src, 0:tok]
            grad_k[:, h] = got[src, tok : 2 * tok]
            grad_v[:, h] = got[src, 2 * tok : 3 * tok]
        grad_q[:, b] = got[2 * c, 3 * tok : 4 * tok]
        grad_k[:, b] = got[2 * c + 1, 3 * tok : 4 * tok]
        grad_v[0:half, b] = got[2 * c, 4 * tok : 4 * tok + half]
        grad_v[half:tok, b] = got[2 * c + 1, 4 * tok : 4 * tok + half]


def temporal_kernel(gains, spatial_terms, own, from_x, from_z, own_out, to_x, to_z, gain_out):
    ins = (own, from_x.at[0], from_z.at[0], from_z.at[1])
    outs = (own_out, to_x.at[0], to_z, to_x.at[1])
    _, pos, width = own.shape
    n = FRAMES * pos
    gain_q, gain_k = gains[2:3, :], gains[3:4, :]
    row = lax.broadcasted_iota(jnp.int32, (n, n), 0)
    col = lax.broadcasted_iota(jnp.int32, (n, n), 1)
    same = lax.rem(row, pos) == lax.rem(col, pos)
    sum_q, sum_k = jnp.zeros((1, D), F32), jnp.zeros((1, D), F32)
    for h in range(width // D):
        at = slice(h * D, (h + 1) * D)
        q, k, v, g = (jnp.concatenate([x[i, :, at] for x in ins], axis=0) for i in range(4))
        inv_q, inv_k = inv_of(q), inv_of(k)
        q_n = (q.astype(F32) * inv_q * gain_q).astype(BF16)
        k_n = (k.astype(F32) * inv_k * gain_k).astype(BF16)
        s = jnp.where(same, dot_t(k_n, q_n) * SCALE, -1e30)
        e = jnp.exp(s - jnp.max(s, axis=0, keepdims=True))
        p = e * (1.0 / jnp.sum(e, axis=0, keepdims=True))
        dp = dot_t(v, g)
        delta = jnp.sum(p * dp, axis=0, keepdims=True)
        ds = (p * (dp - delta) * SCALE).astype(BF16)
        dv = dot(p.astype(BF16), g)
        dk = dot(ds, q_n)
        dq = dot(ds.astype(F32).T.astype(BF16), k_n)
        grad_q, term_q = norm_back(q, inv_q, gain_q, dq)
        grad_k, term_k = norm_back(k, inv_k, gain_k, dk)
        sum_q += term_q
        sum_k += term_k
        for i, x in enumerate((grad_q, grad_k, dv.astype(BF16))):
            for d, out in enumerate(outs):
                out[i, :, at] = x[d * pos : (d + 1) * pos]
    gain_out[...] = spatial_terms[...]
    gain_out[2:3, :] = sum_q
    gain_out[3:4, :] = sum_k


def swap(x, bits, axis="seq"):
    return lax.ppermute(x, axis, [(i, i ^ bits) for i in range(lax.axis_size(axis))])


def add_swapped(x, bits, axis):
    return x + swap(x, bits, axis)


def sum_over(x, axis):
    all_of = jnp.broadcast_to(x[None], (lax.axis_size(axis), *x.shape))
    return jnp.sum(lax.all_to_all(all_of, axis, 0, 0, tiled=True), axis=0)


def local(q_spatial, k_spatial, v_spatial, q_temporal, k_temporal, v_temporal, upstream, norm_gains):
    tok, width = q_spatial.shape[1:]
    nseq = lax.axis_size("seq")
    group = nseq // FRAMES
    n = group * tok
    pos = tok // FRAMES
    at = lax.axis_index("seq").astype(jnp.int32)
    core, frame = at & 1, at // group
    frame_groups = [[f * group + j for j in range(group)] for f in range(FRAMES)]

    def shape(*dims):
        return jax.ShapeDtypeStruct(dims, BF16)

    def exchange(x):
        return lax.all_to_all(x, "seq", 0, 0, axis_index_groups=frame_groups, tiled=True)

    packed = pl.pallas_call(
        spatial_pack_kernel,
        out_shape=shape(group, 6, tok, D),
        in_specs=[HBM] * 4,
        out_specs=HBM,
        scratch_shapes=[
            pltpu.VMEM((group, 6, tok, D), BF16),
            pltpu.SemaphoreType.DMA((group, 6)),
            pltpu.SemaphoreType.DMA((group,)),
        ],
        compiler_params=params(60),
        cost_estimate=pl.CostEstimate(flops=0, bytes_accessed=0, transcendentals=0),
        name="spatial_pack",
    )(q_spatial[0], k_spatial[0], v_spatial[0], upstream[0])
    mine = exchange(packed.reshape(group, 6 * tok, D)).reshape(group, 6, tok, D)
    keep, to_x, to_z = move(
        temporal_pack, "temporal_pack",
        [shape(4, pos, width), shape(2, 4, pos, width), shape(4, pos, width)], [frame],
        q_temporal[0], k_temporal[0], v_temporal[0], upstream[0], src=HBM,
    )
    from_x = swap(to_x, 2 * group)
    (to_z,) = move(forward_pack, "forward_pack", [shape(2, 4, pos, width)], [frame], to_z, from_x)
    mine, to_z = lax.optimization_barrier((mine, to_z))
    from_z = swap(to_z, group)

    other = swap(mine[:, 4:6], 1)
    spatial_grads, spatial_terms = pl.pallas_call(
        spatial_kernel,
        out_shape=(shape(group, 4 * tok + tok // 2, D), jax.ShapeDtypeStruct((8, D), F32)),
        in_specs=[SMEM, VMEM, VMEM, VMEM],
        out_specs=(VMEM, VMEM),
        scratch_shapes=[
            pltpu.VMEM((n, D), BF16),
            pltpu.VMEM((n, D), BF16),
            pltpu.VMEM((D, n), BF16),
            pltpu.VMEM((n, D), BF16),
            pltpu.VMEM((n, D), BF16),
            pltpu.VMEM((n, D), BF16),
            pltpu.VMEM((n, D), BF16),
            pltpu.VMEM((n, D), F32),
            pltpu.VMEM((n, D), F32),
            pltpu.VMEM((n, D), F32),
        ],
        compiler_params=params(),
        cost_estimate=pl.CostEstimate(flops=0, bytes_accessed=0, transcendentals=0),
        name="spatial_backward",
    )(core.reshape(1), norm_gains, mine, other)
    back = exchange(spatial_grads)

    piece = shape(3, pos, width)
    own, to_x, to_z, terms = pl.pallas_call(
        temporal_kernel,
        out_shape=(piece, shape(2, 3, pos, width), piece, jax.ShapeDtypeStruct((8, D), F32)),
        in_specs=[VMEM] * 5,
        out_specs=(VMEM,) * 4,
        compiler_params=params(),
        cost_estimate=pl.CostEstimate(
            flops=10000 * tok * tok * width, bytes_accessed=14 * tok * width, transcendentals=tok * tok * 12
        ),
        name="temporal_backward",
    )(norm_gains, spatial_terms, keep, from_x, from_z)
    back_x = swap(to_x, 2 * group)
    terms = add_swapped(add_swapped(terms, 2, "dp"), 4, "dp")
    to_z, terms = lax.optimization_barrier((to_z, terms))
    (to_z,) = move(forward_pack, "forward_back_pack", [shape(2, 3, pos, width)], [frame], to_z, back_x)
    back_z = swap(to_z, group)
    terms = add_swapped(add_swapped(terms, 8, "dp"), 1, "dp")
    terms, back = lax.optimization_barrier((terms, back))
    gains = sum_over(terms, "seq")[:4]
    grad_qt, grad_kt, grad_vt = move(
        temporal_unpack, "temporal_unpack", [shape(tok, width)] * 3, [frame], own, back_x, back_z, dst=HBM
    )
    grad_qs, grad_ks, grad_vs = pl.pallas_call(
        spatial_unpack_kernel,
        out_shape=(shape(tok, width),) * 3,
        in_specs=[VMEM],
        out_specs=(VMEM,) * 3,
        compiler_params=params(16),
        name="spatial_unpack",
    )(back)
    count = lax.axis_size("dp") * nseq * tok * (width // D)
    gains = gains / jnp.float32(math.sqrt(count))
    return (grad_qs[None], grad_ks[None], grad_vs[None], grad_qt[None], grad_kt[None], grad_vt[None], gains)


def solution(mesh):
    rows = P("dp", "seq", None)
    return jax.shard_map(
        local, mesh=mesh, in_specs=(rows,) * 7 + (P(),), out_specs=(rows,) * 6 + (P(),), check_vma=False
    )
```

```python
import functools
import math

import jax
import jax.numpy as jnp
from jax import lax
from jax.experimental import pallas as pl
from jax.experimental.pallas import tpu as pltpu
from jax.sharding import PartitionSpec as P

D = 128
FRAMES = 4
EPS = 1e-06
SCALE = D**-0.5
F32, BF16 = jnp.float32, jnp.bfloat16
CHIPS = 4
QBLK = 256

VMEM = pl.BlockSpec(memory_space=pltpu.VMEM)
SMEM = pl.BlockSpec(memory_space=pltpu.SMEM)
HBM = pl.BlockSpec(memory_space=pltpu.HBM)


def params(mib=32):
    return pltpu.CompilerParams(vmem_limit_bytes=mib * 2**20)


def dot(a, b):
    return jnp.dot(a, b, preferred_element_type=F32)


def dot_t(a, b):
    return lax.dot_general(a, b, (((1,), (1,)), ((), ())), preferred_element_type=F32)


def inv_of(raw):
    full = raw.astype(F32)
    return lax.rsqrt(jnp.mean(full * full, axis=-1, keepdims=True) + EPS)


def norm_back(raw, inv, gain, grad):
    full = raw.astype(F32)
    scaled = gain * grad
    result = inv * scaled - full * (inv * inv * inv) * jnp.mean(full * scaled, axis=-1, keepdims=True)
    gain_term = jnp.sum(grad * full * inv, axis=0, keepdims=True)
    return result.astype(BF16), gain_term


def cols(head):
    return slice(head * D, (head + 1) * D)


def move(plan, name, outs, scalars, *operands, src=VMEM, dst=VMEM):
    n_in = len(operands)
    inside = src is VMEM and dst is VMEM
    count = len(plan(scalars, [Shape(x) for x in operands], [Shape(x) for x in outs]))

    def kernel(ids, *refs):
        outs_at = n_in + len(outs)
        pairs = plan([ids[i] for i in range(ids.shape[0])], refs[:n_in], refs[n_in:outs_at])
        if inside:
            for a, b in pairs:
                b[...] = a[...]
            return
        copies = [pltpu.make_async_copy(a, b, refs[-1].at[i]) for i, (a, b) in enumerate(pairs)]
        for c in copies:
            c.start()
        for c in copies:
            c.wait()

    return pl.pallas_call(
        kernel,
        out_shape=tuple(outs),
        in_specs=[SMEM] + [src] * n_in,
        out_specs=(dst,) * len(outs),
        scratch_shapes=[] if inside else [pltpu.SemaphoreType.DMA((count,))],
        compiler_params=params(16),
        cost_estimate=pl.CostEstimate(flops=0, bytes_accessed=0, transcendentals=0),
        name=name,
    )(jnp.stack(scalars), *operands)


class Shape:
    def __init__(self, x):
        self.shape = x.shape

    @property
    def at(self):
        return self

    def __getitem__(self, _):
        return self


def quarter(which, pos):
    return pl.ds(pl.multiple_of(which * pos, pos), pos)


def temporal_pack(ids, ins, outs):
    (frame,) = ids
    keep, to_x, to_z = outs
    pos = keep.shape[1]
    places = ((keep, 0), (to_x.at[0], 2), (to_x.at[1], 3), (to_z, 1))
    return [
        (x.at[quarter(frame ^ d, pos)], target.at[i])
        for target, d in places
        for i, x in enumerate(ins)
    ]


def forward_pack(ids, ins, outs):
    mine, from_x = ins
    return [(mine, outs[0].at[0]), (from_x.at[1], outs[0].at[1])]


def temporal_unpack(ids, ins, outs):
    (frame,) = ids
    own, from_x, from_z = ins
    pos = own.shape[1]
    places = ((own, 0), (from_x.at[0], 2), (from_z.at[0], 1), (from_z.at[1], 3))
    return [
        (r.at[i], x.at[quarter(frame ^ d, pos)])
        for r, d in places
        for i, x in enumerate(outs)
    ]


def spatial_pack_kernel(q, k, v, g, out, held, read, write):
    targets = []
    for c in range(CHIPS):
        a, b, e = cols(3 * c), cols(3 * c + 1), cols(3 * c + 2)
        targets.append([(q, a), (k, a), (v, a), (g, a), (q, b), (g, b)])
        targets.append([(q, e), (k, e), (v, e), (g, e), (k, b), (v, b)])
    blocks = [
        [pltpu.make_async_copy(x.at[:, h], held.at[t, i], read.at[t, i]) for i, (x, h) in enumerate(target)]
        for t, target in enumerate(targets)
    ]
    ends = [pltpu.make_async_copy(held.at[t], out.at[t], write.at[t]) for t in range(len(targets))]
    for target in blocks:
        for block in target:
            block.start()
    for target, end in zip(blocks, ends):
        for block in target:
            block.wait()
        end.start()
    for end in ends:
        end.wait()


def spatial_kernel(core_ref, gains, mine, other, out, gain_out, qn, kn, knt, gg, vv, raw_q, raw_k, dq, dk, dv):
    core = core_ref[0]
    n = qn.shape[0]
    srcs = mine.shape[0]
    tok = n // srcs
    gain_q, gain_k = gains[0:1, :], gains[1:2, :]

    def flat(x):
        return x.reshape(n, D)

    def head():
        q, k = raw_q[...], raw_k[...]
        inv_q, inv_k = inv_of(q), inv_of(k)
        qn[...] = (q.astype(F32) * inv_q * gain_q).astype(BF16)
        k_n = (k.astype(F32) * inv_k * gain_k).astype(BF16)
        kn[...] = k_n
        knt[...] = k_n.astype(F32).T.astype(BF16)
        dk[...] = jnp.zeros_like(dk)
        dv[...] = jnp.zeros_like(dv)

        def step(i, carry):
            rows = pl.ds(pl.multiple_of(i * QBLK, QBLK), QBLK)
            qb, gb = qn[rows, :], gg[rows, :]
            s = dot_t(kn[...], qb) * SCALE
            e = jnp.exp(s - jnp.max(s, axis=0, keepdims=True))
            p = e * (1.0 / jnp.sum(e, axis=0, keepdims=True))
            dp = dot_t(vv[...], gb)
            delta = jnp.sum(p * dp, axis=0, keepdims=True)
            ds = (p * (dp - delta) * SCALE).astype(BF16)
            dv[...] += dot(p.astype(BF16), gb)
            dk[...] += dot(ds, qb)
            dq[rows, :] = dot(knt[...], ds).T
            return carry

        lax.fori_loop(0, n // QBLK, step, 0)
        grad_q, term_q = norm_back(q, inv_q, gain_q, dq[...])
        grad_k, term_k = norm_back(k, inv_k, gain_k, dk[...])
        return grad_q, grad_k, dv[...].astype(BF16), term_q, term_k

    def blocks(x):
        return x.reshape(srcs, tok, D)

    raw_q[...] = flat(mine[:, 0])
    raw_k[...] = flat(mine[:, 1])
    vv[...] = flat(mine[:, 2])
    gg[...] = flat(mine[:, 3])
    grad_q, grad_k, grad_v, term_q, term_k = head()
    out[:, 0:tok] = blocks(grad_q)
    out[:, tok : 2 * tok] = blocks(grad_k)
    out[:, 2 * tok : 3 * tok] = blocks(grad_v)
    gain_out[...] = jnp.zeros_like(gain_out)
    gain_out[0:1, :] = term_q
    gain_out[1:2, :] = term_k

    @pl.when(core == 0)
    def _():
        raw_q[...] = flat(mine[:, 4])
        gg[...] = flat(mine[:, 5])
        raw_k[...] = flat(other[:, 0])
        vv[...] = flat(other[:, 1])

    @pl.when(core == 1)
    def _():
        raw_k[...] = flat(mine[:, 4])
        vv[...] = flat(mine[:, 5])
        raw_q[...] = flat(other[:, 0])
        gg[...] = flat(other[:, 1])

    grad_q, grad_k, grad_v, term_q, term_k = head()
    half = tok // 2

    @pl.when(core == 0)
    def _():
        out[:, 3 * tok : 4 * tok] = blocks(grad_q)
        out[:, 4 * tok : 4 * tok + half] = blocks(grad_v)[:, :half]
        gain_out[0:1, :] += term_q

    @pl.when(core == 1)
    def _():
        out[:, 3 * tok : 4 * tok] = blocks(grad_k)
        out[:, 4 * tok : 4 * tok + half] = blocks(grad_v)[:, half:]
        gain_out[1:2, :] += term_k


def spatial_unpack_kernel(got, grad_q, grad_k, grad_v):
    tok = grad_q.shape[0]
    half = tok // 2
    for c in range(CHIPS):
        a, b, e = cols(3 * c), cols(3 * c + 1), cols(3 * c + 2)
        for core, h in ((0, a), (1, e)):
            src = 2 * c + core
            grad_q[:, h] = got[src, 0:tok]
            grad_k[:, h] = got[src, tok : 2 * tok]
            grad_v[:, h] = got[src, 2 * tok : 3 * tok]
        grad_q[:, b] = got[2 * c, 3 * tok : 4 * tok]
        grad_k[:, b] = got[2 * c + 1, 3 * tok : 4 * tok]
        grad_v[0:half, b] = got[2 * c, 4 * tok : 4 * tok + half]
        grad_v[half:tok, b] = got[2 * c + 1, 4 * tok : 4 * tok + half]


def temporal_kernel(gains, spatial_terms, own, from_x, from_z, own_out, to_x, to_z, gain_out):
    ins = (own, from_x.at[0], from_z.at[0], from_z.at[1])
    outs = (own_out, to_x.at[0], to_z, to_x.at[1])
    _, pos, width = own.shape
    n = FRAMES * pos
    gain_q, gain_k = gains[2:3, :], gains[3:4, :]
    row = lax.broadcasted_iota(jnp.int32, (n, n), 0)
    col = lax.broadcasted_iota(jnp.int32, (n, n), 1)
    same = lax.rem(row, pos) == lax.rem(col, pos)
    sum_q, sum_k = jnp.zeros((1, D), F32), jnp.zeros((1, D), F32)
    for h in range(width // D):
        at = slice(h * D, (h + 1) * D)
        q, k, v, g = (jnp.concatenate([x[i, :, at] for x in ins], axis=0) for i in range(4))
        inv_q, inv_k = inv_of(q), inv_of(k)
        q_n = (q.astype(F32) * inv_q * gain_q).astype(BF16)
        k_n = (k.astype(F32) * inv_k * gain_k).astype(BF16)
        s = jnp.where(same, dot_t(k_n, q_n) * SCALE, -1e30)
        e = jnp.exp(s - jnp.max(s, axis=0, keepdims=True))
        p = e * (1.0 / jnp.sum(e, axis=0, keepdims=True))
        dp = dot_t(v, g)
        delta = jnp.sum(p * dp, axis=0, keepdims=True)
        ds = (p * (dp - delta) * SCALE).astype(BF16)
        dv = dot(p.astype(BF16), g)
        dk = dot(ds, q_n)
        dq = dot(ds.astype(F32).T.astype(BF16), k_n)
        grad_q, term_q = norm_back(q, inv_q, gain_q, dq)
        grad_k, term_k = norm_back(k, inv_k, gain_k, dk)
        sum_q += term_q
        sum_k += term_k
        for i, x in enumerate((grad_q, grad_k, dv.astype(BF16))):
            for d, out in enumerate(outs):
                out[i, :, at] = x[d * pos : (d + 1) * pos]
    gain_out[...] = spatial_terms[...]
    gain_out[2:3, :] = sum_q
    gain_out[3:4, :] = sum_k


def swap(x, bits, axis="seq"):
    return lax.ppermute(x, axis, [(i, i ^ bits) for i in range(lax.axis_size(axis))])


def add_swapped(x, bits, axis):
    return x + swap(x, bits, axis)


def sum_over(x, axis):
    all_of = jnp.broadcast_to(x[None], (lax.axis_size(axis), *x.shape))
    return jnp.sum(lax.all_to_all(all_of, axis, 0, 0, tiled=True), axis=0)


def local(q_spatial, k_spatial, v_spatial, q_temporal, k_temporal, v_temporal, upstream, norm_gains):
    tok, width = q_spatial.shape[1:]
    nseq = lax.axis_size("seq")
    group = nseq // FRAMES
    n = group * tok
    pos = tok // FRAMES
    at = lax.axis_index("seq").astype(jnp.int32)
    core, frame = at & 1, at // group
    frame_groups = [[f * group + j for j in range(group)] for f in range(FRAMES)]

    def shape(*dims):
        return jax.ShapeDtypeStruct(dims, BF16)

    def exchange(x):
        return lax.all_to_all(x, "seq", 0, 0, axis_index_groups=frame_groups, tiled=True)

    packed = pl.pallas_call(
        spatial_pack_kernel,
        out_shape=shape(group, 6, tok, D),
        in_specs=[HBM] * 4,
        out_specs=HBM,
        scratch_shapes=[
            pltpu.VMEM((group, 6, tok, D), BF16),
            pltpu.SemaphoreType.DMA((group, 6)),
            pltpu.SemaphoreType.DMA((group,)),
        ],
        compiler_params=params(60),
        cost_estimate=pl.CostEstimate(flops=0, bytes_accessed=0, transcendentals=0),
        name="spatial_pack",
    )(q_spatial[0], k_spatial[0], v_spatial[0], upstream[0])
    mine = exchange(packed.reshape(group, 6 * tok, D)).reshape(group, 6, tok, D)
    keep, to_x, to_z = move(
        temporal_pack, "temporal_pack",
        [shape(4, pos, width), shape(2, 4, pos, width), shape(4, pos, width)], [frame],
        q_temporal[0], k_temporal[0], v_temporal[0], upstream[0], src=HBM,
    )
    from_x = swap(to_x, 2 * group)
    (to_z,) = move(forward_pack, "forward_pack", [shape(2, 4, pos, width)], [frame], to_z, from_x)
    mine, to_z = lax.optimization_barrier((mine, to_z))
    from_z = swap(to_z, group)

    other = swap(mine[:, 4:6], 1)
    spatial_grads, spatial_terms = pl.pallas_call(
        spatial_kernel,
        out_shape=(shape(group, 4 * tok + tok // 2, D), jax.ShapeDtypeStruct((8, D), F32)),
        in_specs=[SMEM, VMEM, VMEM, VMEM],
        out_specs=(VMEM, VMEM),
        scratch_shapes=[
            pltpu.VMEM((n, D), BF16),
            pltpu.VMEM((n, D), BF16),
            pltpu.VMEM((D, n), BF16),
            pltpu.VMEM((n, D), BF16),
            pltpu.VMEM((n, D), BF16),
            pltpu.VMEM((n, D), BF16),
            pltpu.VMEM((n, D), BF16),
            pltpu.VMEM((n, D), F32),
            pltpu.VMEM((n, D), F32),
            pltpu.VMEM((n, D), F32),
        ],
        compiler_params=params(),
        cost_estimate=pl.CostEstimate(flops=0, bytes_accessed=0, transcendentals=0),
        name="spatial_backward",
    )(core.reshape(1), norm_gains, mine, other)
    back = exchange(spatial_grads)

    piece = shape(3, pos, width)
    own, to_x, to_z, terms = pl.pallas_call(
        temporal_kernel,
        out_shape=(piece, shape(2, 3, pos, width), piece, jax.ShapeDtypeStruct((8, D), F32)),
        in_specs=[VMEM] * 5,
        out_specs=(VMEM,) * 4,
        compiler_params=params(),
        cost_estimate=pl.CostEstimate(
            flops=10000 * tok * tok * width, bytes_accessed=14 * tok * width, transcendentals=tok * tok * 12
        ),
        name="temporal_backward",
    )(norm_gains, spatial_terms, keep, from_x, from_z)
    back_x = swap(to_x, 2 * group)
    for bits in (2, 4, 1):
        terms = add_swapped(terms, bits, "dp")
    to_z, terms = lax.optimization_barrier((to_z, terms))
    (to_z,) = move(forward_pack, "forward_back_pack", [shape(2, 3, pos, width)], [frame], to_z, back_x)
    back_z = swap(to_z, group)
    terms = add_swapped(terms, 8, "dp")
    terms, back = lax.optimization_barrier((terms, back))
    gains = sum_over(terms, "seq")[:4]
    grad_qt, grad_kt, grad_vt = move(
        temporal_unpack, "temporal_unpack", [shape(tok, width)] * 3, [frame], own, back_x, back_z, dst=HBM
    )
    grad_qs, grad_ks, grad_vs = pl.pallas_call(
        spatial_unpack_kernel,
        out_shape=(shape(tok, width),) * 3,
        in_specs=[VMEM],
        out_specs=(VMEM,) * 3,
        compiler_params=params(16),
        name="spatial_unpack",
    )(back)
    count = lax.axis_size("dp") * nseq * tok * (width // D)
    gains = gains / jnp.float32(math.sqrt(count))
    return (grad_qs[None], grad_ks[None], grad_vs[None], grad_qt[None], grad_kt[None], grad_vt[None], gains)


def solution(mesh):
    rows = P("dp", "seq", None)
    return jax.shard_map(
        local, mesh=mesh, in_specs=(rows,) * 7 + (P(),), out_specs=(rows,) * 6 + (P(),), check_vma=False
    )
```

```python
import functools
import math

import jax
import jax.numpy as jnp
from jax import lax
from jax.experimental import pallas as pl
from jax.experimental.pallas import tpu as pltpu
from jax.sharding import PartitionSpec as P

D = 128
FRAMES = 4
EPS = 1e-06
SCALE = D**-0.5
F32, BF16 = jnp.float32, jnp.bfloat16
CHIPS = 4
QBLK = 256

VMEM = pl.BlockSpec(memory_space=pltpu.VMEM)
SMEM = pl.BlockSpec(memory_space=pltpu.SMEM)
HBM = pl.BlockSpec(memory_space=pltpu.HBM)


def params(mib=32):
    return pltpu.CompilerParams(vmem_limit_bytes=mib * 2**20)


def dot(a, b):
    return jnp.dot(a, b, preferred_element_type=F32)


def dot_t(a, b):
    return lax.dot_general(a, b, (((1,), (1,)), ((), ())), preferred_element_type=F32)


def inv_of(raw):
    full = raw.astype(F32)
    return lax.rsqrt(jnp.mean(full * full, axis=-1, keepdims=True) + EPS)


def norm_back(raw, inv, gain, grad):
    full = raw.astype(F32)
    scaled = gain * grad
    result = inv * scaled - full * (inv * inv * inv) * jnp.mean(full * scaled, axis=-1, keepdims=True)
    gain_term = jnp.sum(grad * full * inv, axis=0, keepdims=True)
    return result.astype(BF16), gain_term


def cols(head):
    return slice(head * D, (head + 1) * D)


def move(plan, name, outs, scalars, *operands, src=VMEM, dst=VMEM):
    n_in = len(operands)
    inside = src is VMEM and dst is VMEM
    count = len(plan(scalars, [Shape(x) for x in operands], [Shape(x) for x in outs]))

    def kernel(ids, *refs):
        outs_at = n_in + len(outs)
        pairs = plan([ids[i] for i in range(ids.shape[0])], refs[:n_in], refs[n_in:outs_at])
        if inside:
            for a, b in pairs:
                b[...] = a[...]
            return
        copies = [pltpu.make_async_copy(a, b, refs[-1].at[i]) for i, (a, b) in enumerate(pairs)]
        for c in copies:
            c.start()
        for c in copies:
            c.wait()

    return pl.pallas_call(
        kernel,
        out_shape=tuple(outs),
        in_specs=[SMEM] + [src] * n_in,
        out_specs=(dst,) * len(outs),
        scratch_shapes=[] if inside else [pltpu.SemaphoreType.DMA((count,))],
        compiler_params=params(16),
        cost_estimate=pl.CostEstimate(flops=0, bytes_accessed=0, transcendentals=0),
        name=name,
    )(jnp.stack(scalars), *operands)


class Shape:
    def __init__(self, x):
        self.shape = x.shape

    @property
    def at(self):
        return self

    def __getitem__(self, _):
        return self


def quarter(which, pos):
    return pl.ds(pl.multiple_of(which * pos, pos), pos)


def temporal_pack(ids, ins, outs):
    (frame,) = ids
    keep, to_x, to_z = outs
    pos = keep.shape[1]
    places = ((keep, 0), (to_x.at[0], 2), (to_x.at[1], 3), (to_z, 1))
    return [
        (x.at[quarter(frame ^ d, pos)], target.at[i])
        for target, d in places
        for i, x in enumerate(ins)
    ]


def forward_pack(ids, ins, outs):
    mine, from_x = ins
    return [(mine, outs[0].at[0]), (from_x.at[1], outs[0].at[1])]


def temporal_unpack(ids, ins, outs):
    (frame,) = ids
    own, from_x, from_z = ins
    pos = own.shape[1]
    places = ((own, 0), (from_x.at[0], 2), (from_z.at[0], 1), (from_z.at[1], 3))
    return [
        (r.at[i], x.at[quarter(frame ^ d, pos)])
        for r, d in places
        for i, x in enumerate(outs)
    ]


def spatial_pack_kernel(q, k, v, g, out, held, read, write):
    targets = []
    for c in range(CHIPS):
        a, b, e = cols(3 * c), cols(3 * c + 1), cols(3 * c + 2)
        targets.append([(q, a), (k, a), (v, a), (g, a), (q, b), (g, b)])
        targets.append([(q, e), (k, e), (v, e), (g, e), (k, b), (v, b)])
    blocks = [
        [pltpu.make_async_copy(x.at[:, h], held.at[t, i], read.at[t, i]) for i, (x, h) in enumerate(target)]
        for t, target in enumerate(targets)
    ]
    ends = [pltpu.make_async_copy(held.at[t], out.at[t], write.at[t]) for t in range(len(targets))]
    for target in blocks:
        for block in target:
            block.start()
    for target, end in zip(blocks, ends):
        for block in target:
            block.wait()
        end.start()
    for end in ends:
        end.wait()


def spatial_kernel(core_ref, gains, mine, other, out, gain_out, qn, kn, knt, gg, vv, raw_q, raw_k, dq, dk, dv):
    core = core_ref[0]
    n = qn.shape[0]
    srcs = mine.shape[0]
    tok = n // srcs
    gain_q, gain_k = gains[0:1, :], gains[1:2, :]

    def flat(x):
        return x.reshape(n, D)

    def head():
        q, k = raw_q[...], raw_k[...]
        inv_q, inv_k = inv_of(q), inv_of(k)
        qn[...] = (q.astype(F32) * inv_q * gain_q).astype(BF16)
        k_n = (k.astype(F32) * inv_k * gain_k).astype(BF16)
        kn[...] = k_n
        knt[...] = k_n.astype(F32).T.astype(BF16)
        dk[...] = jnp.zeros_like(dk)
        dv[...] = jnp.zeros_like(dv)

        def step(i, carry):
            rows = pl.ds(pl.multiple_of(i * QBLK, QBLK), QBLK)
            qb, gb = qn[rows, :], gg[rows, :]
            s = dot_t(kn[...], qb) * SCALE
            e = jnp.exp(s - jnp.max(s, axis=0, keepdims=True))
            p = e * (1.0 / jnp.sum(e, axis=0, keepdims=True))
            dp = dot_t(vv[...], gb)
            delta = jnp.sum(p * dp, axis=0, keepdims=True)
            ds = (p * (dp - delta) * SCALE).astype(BF16)
            dv[...] += dot(p.astype(BF16), gb)
            dk[...] += dot(ds, qb)
            dq[rows, :] = dot(knt[...], ds).T
            return carry

        lax.fori_loop(0, n // QBLK, step, 0)
        grad_q, term_q = norm_back(q, inv_q, gain_q, dq[...])
        grad_k, term_k = norm_back(k, inv_k, gain_k, dk[...])
        return grad_q, grad_k, dv[...].astype(BF16), term_q, term_k

    def blocks(x):
        return x.reshape(srcs, tok, D)

    raw_q[...] = flat(mine[:, 0])
    raw_k[...] = flat(mine[:, 1])
    vv[...] = flat(mine[:, 2])
    gg[...] = flat(mine[:, 3])
    grad_q, grad_k, grad_v, term_q, term_k = head()
    out[:, 0:tok] = blocks(grad_q)
    out[:, tok : 2 * tok] = blocks(grad_k)
    out[:, 2 * tok : 3 * tok] = blocks(grad_v)
    gain_out[...] = jnp.zeros_like(gain_out)
    gain_out[0:1, :] = term_q
    gain_out[1:2, :] = term_k

    @pl.when(core == 0)
    def _():
        raw_q[...] = flat(mine[:, 4])
        gg[...] = flat(mine[:, 5])
        raw_k[...] = flat(other[:, 0])
        vv[...] = flat(other[:, 1])

    @pl.when(core == 1)
    def _():
        raw_k[...] = flat(mine[:, 4])
        vv[...] = flat(mine[:, 5])
        raw_q[...] = flat(other[:, 0])
        gg[...] = flat(other[:, 1])

    grad_q, grad_k, grad_v, term_q, term_k = head()
    half = tok // 2

    @pl.when(core == 0)
    def _():
        out[:, 3 * tok : 4 * tok] = blocks(grad_q)
        out[:, 4 * tok : 4 * tok + half] = blocks(grad_v)[:, :half]
        gain_out[0:1, :] += term_q

    @pl.when(core == 1)
    def _():
        out[:, 3 * tok : 4 * tok] = blocks(grad_k)
        out[:, 4 * tok : 4 * tok + half] = blocks(grad_v)[:, half:]
        gain_out[1:2, :] += term_k


def spatial_unpack_kernel(got, grad_q, grad_k, grad_v):
    tok = grad_q.shape[0]
    half = tok // 2
    for c in range(CHIPS):
        a, b, e = cols(3 * c), cols(3 * c + 1), cols(3 * c + 2)
        for core, h in ((0, a), (1, e)):
            src = 2 * c + core
            grad_q[:, h] = got[src, 0:tok]
            grad_k[:, h] = got[src, tok : 2 * tok]
            grad_v[:, h] = got[src, 2 * tok : 3 * tok]
        grad_q[:, b] = got[2 * c, 3 * tok : 4 * tok]
        grad_k[:, b] = got[2 * c + 1, 3 * tok : 4 * tok]
        grad_v[0:half, b] = got[2 * c, 4 * tok : 4 * tok + half]
        grad_v[half:tok, b] = got[2 * c + 1, 4 * tok : 4 * tok + half]


def temporal_kernel(gains, spatial_terms, own, from_x, from_z, own_out, to_x, to_z, gain_out):
    ins = (own, from_x.at[0], from_z.at[0], from_z.at[1])
    outs = (own_out, to_x.at[0], to_z, to_x.at[1])
    _, pos, width = own.shape
    n = FRAMES * pos
    gain_q, gain_k = gains[2:3, :], gains[3:4, :]
    row = lax.broadcasted_iota(jnp.int32, (n, n), 0)
    col = lax.broadcasted_iota(jnp.int32, (n, n), 1)
    same = lax.rem(row, pos) == lax.rem(col, pos)
    sum_q, sum_k = jnp.zeros((1, D), F32), jnp.zeros((1, D), F32)
    for h in range(width // D):
        at = slice(h * D, (h + 1) * D)
        q, k, v, g = (jnp.concatenate([x[i, :, at] for x in ins], axis=0) for i in range(4))
        inv_q, inv_k = inv_of(q), inv_of(k)
        q_n = (q.astype(F32) * inv_q * gain_q).astype(BF16)
        k_n = (k.astype(F32) * inv_k * gain_k).astype(BF16)
        s = jnp.where(same, dot_t(k_n, q_n) * SCALE, -1e30)
        e = jnp.exp(s - jnp.max(s, axis=0, keepdims=True))
        p = e * (1.0 / jnp.sum(e, axis=0, keepdims=True))
        dp = dot_t(v, g)
        delta = jnp.sum(p * dp, axis=0, keepdims=True)
        ds = (p * (dp - delta) * SCALE).astype(BF16)
        dv = dot(p.astype(BF16), g)
        dk = dot(ds, q_n)
        dq = dot(ds.astype(F32).T.astype(BF16), k_n)
        grad_q, term_q = norm_back(q, inv_q, gain_q, dq)
        grad_k, term_k = norm_back(k, inv_k, gain_k, dk)
        sum_q += term_q
        sum_k += term_k
        for i, x in enumerate((grad_q, grad_k, dv.astype(BF16))):
            for d, out in enumerate(outs):
                out[i, :, at] = x[d * pos : (d + 1) * pos]
    gain_out[...] = spatial_terms[...]
    gain_out[2:3, :] = sum_q
    gain_out[3:4, :] = sum_k


def swap(x, bits, axis="seq"):
    return lax.ppermute(x, axis, [(i, i ^ bits) for i in range(lax.axis_size(axis))])


def add_swapped(x, bits, axis):
    return x + swap(x, bits, axis)


def sum_over(x, axis):
    all_of = jnp.broadcast_to(x[None], (lax.axis_size(axis), *x.shape))
    return jnp.sum(lax.all_to_all(all_of, axis, 0, 0, tiled=True), axis=0)


def local(q_spatial, k_spatial, v_spatial, q_temporal, k_temporal, v_temporal, upstream, norm_gains):
    tok, width = q_spatial.shape[1:]
    nseq = lax.axis_size("seq")
    group = nseq // FRAMES
    n = group * tok
    pos = tok // FRAMES
    at = lax.axis_index("seq").astype(jnp.int32)
    core, frame = at & 1, at // group
    frame_groups = [[f * group + j for j in range(group)] for f in range(FRAMES)]

    def shape(*dims):
        return jax.ShapeDtypeStruct(dims, BF16)

    def exchange(x):
        return lax.all_to_all(x, "seq", 0, 0, axis_index_groups=frame_groups, tiled=True)

    packed = pl.pallas_call(
        spatial_pack_kernel,
        out_shape=shape(group, 6, tok, D),
        in_specs=[HBM] * 4,
        out_specs=HBM,
        scratch_shapes=[
            pltpu.VMEM((group, 6, tok, D), BF16),
            pltpu.SemaphoreType.DMA((group, 6)),
            pltpu.SemaphoreType.DMA((group,)),
        ],
        compiler_params=params(60),
        cost_estimate=pl.CostEstimate(flops=0, bytes_accessed=0, transcendentals=0),
        name="spatial_pack",
    )(q_spatial[0], k_spatial[0], v_spatial[0], upstream[0])
    mine = exchange(packed.reshape(group, 6 * tok, D)).reshape(group, 6, tok, D)
    keep, to_x, to_z = move(
        temporal_pack, "temporal_pack",
        [shape(4, pos, width), shape(2, 4, pos, width), shape(4, pos, width)], [frame],
        q_temporal[0], k_temporal[0], v_temporal[0], upstream[0], src=HBM,
    )
    from_x = swap(to_x, 2 * group)
    (to_z,) = move(forward_pack, "forward_pack", [shape(2, 4, pos, width)], [frame], to_z, from_x)
    mine, to_z = lax.optimization_barrier((mine, to_z))
    from_z = swap(to_z, group)

    other = swap(mine[:, 4:6], 1)
    spatial_grads, spatial_terms = pl.pallas_call(
        spatial_kernel,
        out_shape=(shape(group, 4 * tok + tok // 2, D), jax.ShapeDtypeStruct((8, D), F32)),
        in_specs=[SMEM, VMEM, VMEM, VMEM],
        out_specs=(VMEM, VMEM),
        scratch_shapes=[
            pltpu.VMEM((n, D), BF16),
            pltpu.VMEM((n, D), BF16),
            pltpu.VMEM((D, n), BF16),
            pltpu.VMEM((n, D), BF16),
            pltpu.VMEM((n, D), BF16),
            pltpu.VMEM((n, D), BF16),
            pltpu.VMEM((n, D), BF16),
            pltpu.VMEM((n, D), F32),
            pltpu.VMEM((n, D), F32),
            pltpu.VMEM((n, D), F32),
        ],
        compiler_params=params(),
        cost_estimate=pl.CostEstimate(flops=0, bytes_accessed=0, transcendentals=0),
        name="spatial_backward",
    )(core.reshape(1), norm_gains, mine, other)
    spatial_grads, temporal_gains = lax.optimization_barrier((spatial_grads, norm_gains))
    for _ in range(2):
        temporal_gains = swap(temporal_gains, 1)
    spatial_grads, temporal_gains = lax.optimization_barrier((spatial_grads, temporal_gains))
    back = exchange(spatial_grads)

    piece = shape(3, pos, width)
    own, to_x, to_z, terms = pl.pallas_call(
        temporal_kernel,
        out_shape=(piece, shape(2, 3, pos, width), piece, jax.ShapeDtypeStruct((8, D), F32)),
        in_specs=[VMEM] * 5,
        out_specs=(VMEM,) * 4,
        compiler_params=params(),
        cost_estimate=pl.CostEstimate(
            flops=10000 * tok * tok * width, bytes_accessed=14 * tok * width, transcendentals=tok * tok * 12
        ),
        name="temporal_backward",
    )(temporal_gains, spatial_terms, keep, from_x, from_z)
    back_x = swap(to_x, 2 * group)
    for bits in (2, 4, 1):
        terms = add_swapped(terms, bits, "dp")
    to_z, terms = lax.optimization_barrier((to_z, terms))
    (to_z,) = move(forward_pack, "forward_back_pack", [shape(2, 3, pos, width)], [frame], to_z, back_x)
    back_z = swap(to_z, group)
    terms = add_swapped(terms, 8, "dp")
    terms, back = lax.optimization_barrier((terms, back))
    gains = sum_over(terms, "seq")[:4]
    grad_qt, grad_kt, grad_vt = move(
        temporal_unpack, "temporal_unpack", [shape(tok, width)] * 3, [frame], own, back_x, back_z, dst=HBM
    )
    grad_qs, grad_ks, grad_vs = pl.pallas_call(
        spatial_unpack_kernel,
        out_shape=(shape(tok, width),) * 3,
        in_specs=[VMEM],
        out_specs=(VMEM,) * 3,
        compiler_params=params(16),
        name="spatial_unpack",
    )(back)
    count = lax.axis_size("dp") * nseq * tok * (width // D)
    gains = gains / jnp.float32(math.sqrt(count))
    return (grad_qs[None], grad_ks[None], grad_vs[None], grad_qt[None], grad_kt[None], grad_vt[None], gains)


def solution(mesh):
    rows = P("dp", "seq", None)
    return jax.shard_map(
        local, mesh=mesh, in_specs=(rows,) * 7 + (P(),), out_specs=(rows,) * 6 + (P(),), check_vma=False
    )
```
